128 devices in a mesh: dp: 32 (over x, z, core), head: 4 (over y).
Axes of the slice: x: 4, y: 4, z: 4, core: 2. Of those that a mesh axis runs over, the one named last changes fastest.
Arguments:
- tokens: bfloat16 [12288, 3072], P('dp'), may hold values from -6 to 6
- tile_anchor: int32 [32, 3], P('dp'), may hold values from 0 to 71, as said below
- partners: int32 [32, 12], P('dp'), may hold values from -1 to 31, as said below
- weight: float32 [3072, 12, 3, 128], P('dp', 'head'), may hold values from -0.109375 to 0.109375
- mod_shift: float32 [3072], replicated, may hold values from -3 to 3
- mod_scale: float32 [3072], replicated, may hold values from -2.5 to 2.5
- q_gain: float32 [128], replicated, may hold values from 0.1 to 1.9
- k_gain: float32 [128], replicated, may hold values from 0.1 to 1.9
- grad_out: bfloat16 [12288, 12, 128], P('dp', 'head'), may hold values from -6 to 6
Outputs:
- attn_out: bfloat16 [12288, 12, 128], P('dp', 'head')
- grad_tokens: bfloat16 [12288, 3072], P(('dp', 'head'))
- grad_weight: float32 [3072, 12, 3, 128], P('dp', 'head')
The draws below stay inside these ranges and needn't reach their ends.
Inputs may be any that keep to these rules, and one draw needn't show every extreme that they name: Tile i of the slab has tile coordinates (t, h, w) with i = (w * 2 + t) * 2 + h, and tile_anchor[i] = (t * (6 + frame_gap), corner + h * (8 + row_gap), 15 + w * 8) with corner from 0 to 15, frame_gap from 0 to 15 and row_gap from 0 to min(8, 48), each one number per draw. `partners`: row i lists distinct tiles whose tile coordinates differ from tile i's by at most one in each of the three dimensions; tile i itself comes first; the listed tiles come before every -1; some row lists all such tiles.
All inputs are finite; a program needn't handle non-finite values.
Results may differ from the reference program's by a relative error of at most 0.025.
Values may be sent and summed in bfloat16 or wider, within the bound.
No kernel may reach another device: no remote copies, remote signals or barrier semaphores. Data moves between devices by JAX's collectives and lax.ppermute only.
A program may use at most 128 MiB of HBM per device.

```python
import math
import jax
import jax.numpy as jnp
from jax import lax

D = 3072
HEADS = 12
HEAD_DIM = 128
TT = 6
TH = 8
TW = 8
GT = 2
GH = 2
KMAX = 12
GW = 8
TOKENS = 12288


def draw_partners(key, part):
    key = jax.random.fold_in(key, 11)
    roll_key, pick_key = jax.random.split(key)
    tile_count = GT * GH * GW
    tile_ids = jnp.arange(tile_count, dtype=jnp.int32)
    coord_h = tile_ids % GH
    coord_t = tile_ids // GH % GT
    coord_w = tile_ids // (GT * GH)
    offsets = jnp.arange(27, dtype=jnp.int32)
    near_w = coord_w[:, None] + (offsets // 9 - 1)[None, :]
    near_t = coord_t[:, None] + (offsets // 3 % 3 - 1)[None, :]
    near_h = coord_h[:, None] + (offsets % 3 - 1)[None, :]
    inside = (near_w >= 0) & (near_w < GW) & (near_t >= 0) & (near_t < GT) & (near_h >= 0) & (near_h < GH)
    neighbour = (near_w * GT + near_t) * GH + near_h
    rolls = jax.random.randint(roll_key, (tile_count, 27), 0, 100)
    picks = jax.random.randint(pick_key, (3,), 0, 1000)
    full_w = jnp.minimum(1 + picks[0] % max(GW - 2, 1), GW - 1)
    full_tile = (full_w * GT + picks[1] % GT) * GH + picks[2] % GH
    self_slot = offsets[None, :] == 13
    chosen = inside & ((rolls < 45) | (tile_ids[:, None] == full_tile) | self_slot)
    order_keys = jnp.where(self_slot, -1, jnp.where(chosen, offsets[None, :], 100 + offsets[None, :]))
    ordering = jnp.argsort(order_keys, axis=1)[:, :KMAX]
    listed = jnp.where(chosen, neighbour, -1)
    return jnp.take_along_axis(listed, ordering, axis=1).astype(jnp.int32)


def draw_tile_anchor(key, part):
    key = jax.random.fold_in(key, 12)
    corner_key, frame_key, row_key = jax.random.split(key, 3)
    corner = jax.random.randint(corner_key, (), 0, 16)
    frame_gap = jax.random.randint(frame_key, (), 0, 16)
    row_room = min(8, (GW - 1) * TW - (GH - 1) * TH)
    row_gap = jax.random.randint(row_key, (), 0, row_room + 1)
    tile_ids = jnp.arange(GT * GH * GW, dtype=jnp.int32)
    coord_h = tile_ids % GH
    coord_t = tile_ids // GH % GT
    coord_w = tile_ids // (GT * GH)
    anchor = jnp.stack([coord_t * (TT + frame_gap), corner + coord_h * (TH + row_gap), 15 + coord_w * TW], axis=1)
    return anchor.astype(jnp.int32)


def shard_levels(key, dims, cuts, least, high):
    level, own = 1.0, jax.random.fold_in(key, 6)
    for axis_at, shards_of in cuts:
        steps = jnp.exp(jax.random.uniform(jax.random.fold_in(own, axis_at), (shards_of,), jnp.float32, least / len(cuts), high / len(cuts)))
        level = level * jnp.repeat(steps, dims[axis_at] // shards_of).reshape([-1 if axis == axis_at else 1 for axis in range(len(dims))])
    return level


def noise(rng, shape, spread, reach, shards=(), kind=jnp.bfloat16):
    loudness = shard_levels(rng, shape, shards, -0.22, 0.18) if shards else 1.0
    drawn = jax.random.normal(rng, shape, jnp.float32) * spread * loudness
    return jnp.minimum(jnp.maximum(drawn, -reach), reach).astype(kind)


def setup_inputs(seed: int = 0) -> dict:
    key_list = jax.random.split(jax.random.key(seed), 10)
    tokens = noise(key_list[0], (TOKENS, D), 1.0, 6.0, ((0, 32),))
    tile_anchor = draw_tile_anchor(jax.random.fold_in(key_list[9], 71), 0)
    partners = draw_partners(jax.random.fold_in(key_list[9], 71), 0)
    weight = noise(key_list[3], (D, HEADS, 3, HEAD_DIM), D ** -0.5, 0.109375, ((0, 32), (1, 4)), jnp.float32)
    mod_shift = noise(key_list[4], (D,), 0.5, 3.0, (), jnp.float32)
    mod_scale = noise(key_list[5], (D,), 0.3, 2.5, (), jnp.float32)
    q_gain = jnp.clip(1.0 + 0.18 * jax.random.normal(key_list[6], (HEAD_DIM,), jnp.float32), 0.1, 1.9)
    k_gain = jnp.clip(1.0 + 0.18 * jax.random.normal(key_list[7], (HEAD_DIM,), jnp.float32), 0.1, 1.9)
    grad_out = noise(key_list[8], (TOKENS, HEADS, HEAD_DIM), 1.0, 6.0, ((0, 32), (1, 4)))
    return {"tokens": tokens, "tile_anchor": tile_anchor, "partners": partners, "weight": weight, "mod_shift": mod_shift, "mod_scale": mod_scale, "q_gain": q_gain, "k_gain": k_gain, "grad_out": grad_out}


THETA = 256.0
EPS = 1e-06
HIGH = lax.Precision.HIGHEST

def rope_tables(anchor, head_dim):
    token_ids = jnp.arange(TT * TH * TW, dtype=jnp.int32)
    frames = anchor[0] + token_ids // (TH * TW)
    image_rows = anchor[1] + token_ids // TW % TH
    image_cols = anchor[2] + token_ids % TW
    places = jnp.stack([frames, image_rows, image_cols], axis=1).astype(jnp.float32)
    section_t = head_dim // 8
    section_s = (head_dim - section_t) // 2
    channel = jnp.arange(head_dim, dtype=jnp.int32)
    section_id = jnp.where(channel < section_t, 0, jnp.where(channel < section_t + section_s, 1, 2))
    section_start = jnp.where(section_id == 0, 0, jnp.where(section_id == 1, section_t, section_t + section_s))
    section_len = jnp.where(section_id == 0, section_t, section_s)
    pair_index = ((channel - section_start) // 2).astype(jnp.float32)
    frequency = THETA ** (-2.0 * pair_index / section_len.astype(jnp.float32))
    selector = (section_id[None, :] == jnp.arange(3, dtype=jnp.int32)[:, None]).astype(jnp.float32)
    position_sel = jnp.dot(places, selector, precision=HIGH)
    angles = position_sel * frequency[None, :]
    return (jnp.cos(angles), jnp.sin(angles))

def rotate_pairs(values, cosine, sine_table):
    halves = values.reshape(values.shape[:-1] + (values.shape[-1] // 2, 2))
    turned = jnp.stack([-halves[..., 1], halves[..., 0]], axis=-1).reshape(values.shape)
    return values * cosine[:, None, :] + turned * sine_table[:, None, :]

def prepare(projected, cosine, sine_table, q_gain, k_gain):
    queries = projected[:, :, 0, :]
    keys_raw = projected[:, :, 1, :]
    values_raw = projected[:, :, 2, :]
    queries = queries * lax.rsqrt(lax.optimization_barrier(jnp.mean(queries * queries, axis=-1, keepdims=True)) + EPS) * q_gain
    keys_raw = keys_raw * lax.rsqrt(lax.optimization_barrier(jnp.mean(keys_raw * keys_raw, axis=-1, keepdims=True)) + EPS) * k_gain
    return (rotate_pairs(queries, cosine, sine_table), rotate_pairs(keys_raw, cosine, sine_table), values_raw)

def normalize(tokens, mod_shift, mod_scale):
    floats = tokens.astype(jnp.float32)
    centred = floats - lax.optimization_barrier(jnp.mean(floats, axis=-1, keepdims=True))
    inverse = lax.rsqrt(lax.optimization_barrier(jnp.mean(centred * centred, axis=-1, keepdims=True)) + EPS)
    unit_rows = centred * inverse
    normed = (unit_rows * (1.0 + mod_scale) + mod_shift).astype(jnp.bfloat16)
    return (unit_rows, inverse, normed)

def norm_backward(grad_normed, unit_rows, inverse, mod_scale):
    scaled = grad_normed * (1.0 + mod_scale)
    centred = scaled - lax.optimization_barrier(jnp.mean(scaled, axis=-1, keepdims=True))
    return inverse * (centred - unit_rows * lax.optimization_barrier(jnp.mean(scaled * unit_rows, axis=-1, keepdims=True)))

def bf16_round(values):
    return lax.optimization_barrier(values.astype(jnp.bfloat16)).astype(jnp.float32)

def reference(tokens, tile_anchor, partners, weight, mod_shift, mod_scale, q_gain, k_gain, grad_out):
    token_count, feature_count = tokens.shape
    tile_count = partners.shape[0]
    tile_len = token_count // tile_count
    head_count, head_dim = (weight.shape[1], weight.shape[3])
    columns = head_count * 3 * head_dim
    score_scale = 1.0 / math.sqrt(head_dim)
    unit_rows, inverse, normed = normalize(tokens, mod_shift, mod_scale)
    w_bf = weight.reshape(feature_count, columns).astype(jnp.bfloat16)
    projected = jnp.dot(normed, w_bf, preferred_element_type=jnp.float32).reshape(token_count, head_count, 3, head_dim)
    cosine, sine_table = jax.vmap(lambda anchor: rope_tables(anchor, head_dim))(tile_anchor)
    cosine = cosine.reshape(token_count, head_dim)
    sine_table = sine_table.reshape(token_count, head_dim)
    (queries, keys_all, values_all), pullback = jax.vjp(lambda proj_rows: prepare(proj_rows, cosine, sine_table, q_gain, k_gain), projected)
    tiled = (tile_count, tile_len, head_count, head_dim)
    query_f = bf16_round(queries).reshape(tiled)
    key_f = bf16_round(keys_all).reshape(tiled)
    value_f = bf16_round(values_all).reshape(tiled)
    safe_ids = jnp.where(partners >= 0, partners, 0).astype(jnp.int32)
    valid = (partners >= 0).astype(jnp.float32)

    def tile_weights(tile_index):
        key_block = key_f[safe_ids[tile_index]]
        value_block = value_f[safe_ids[tile_index]]
        logits = jnp.einsum('qhd,jkhd->hqjk', query_f[tile_index], key_block, precision=HIGH) * score_scale
        return (jnp.exp(logits) * valid[tile_index][None, None, :, None], key_block, value_block)

    def forward_tile(tile_index):
        exp_block, key_block, value_block = tile_weights(tile_index)
        denominator = lax.optimization_barrier(jnp.sum(exp_block, axis=(2, 3)))
        numerator = jnp.einsum('hqjk,jkhd->hqd', bf16_round(exp_block), value_block, precision=HIGH)
        return ((numerator / denominator[..., None]).transpose(1, 0, 2).astype(jnp.bfloat16), denominator)
    attn_tiles, denominators = lax.map(forward_tile, jnp.arange(tile_count, dtype=jnp.int32))
    grad_tiles = grad_out.astype(jnp.float32).reshape(tiled)
    deltas = lax.optimization_barrier(jnp.sum(grad_tiles * attn_tiles.astype(jnp.float32), axis=-1))

    def backward_tile(accumulated, tile_index):
        key_acc, value_acc = accumulated
        exp_block, key_block, value_block = tile_weights(tile_index)
        probability = exp_block / denominators[tile_index][:, :, None, None]
        grad_rows = grad_tiles[tile_index]
        value_part = bf16_round(jnp.einsum('hqjk,qhd->jkhd', bf16_round(probability), grad_rows, precision=HIGH))
        grad_prob = jnp.einsum('qhd,jkhd->hqjk', grad_rows, value_block, precision=HIGH)
        dscore = bf16_round(probability * (grad_prob - deltas[tile_index].T[:, :, None, None]))
        grad_query = jnp.einsum('hqjk,jkhd->qhd', dscore, key_block, precision=HIGH) * score_scale
        key_part = bf16_round(jnp.einsum('hqjk,qhd->jkhd', dscore, query_f[tile_index], precision=HIGH) * score_scale)
        targets = jnp.where(partners[tile_index] >= 0, partners[tile_index], tile_count).astype(jnp.int32)
        key_acc = key_acc.at[targets].add(key_part, mode='drop')
        value_acc = value_acc.at[targets].add(value_part, mode='drop')
        return ((key_acc, value_acc), grad_query)
    empty_grads = jnp.zeros(tiled, jnp.float32)
    sums, query_grads = lax.scan(backward_tile, (empty_grads, empty_grads), jnp.arange(tile_count, dtype=jnp.int32))
    flat = (token_count, head_count, head_dim)
    grad_projected = pullback((query_grads.reshape(flat), sums[0].reshape(flat), sums[1].reshape(flat)))[0]
    grad_proj_b = grad_projected.astype(jnp.bfloat16).reshape(token_count, columns)
    normed_tiles = normed.reshape(tile_count, tile_len, feature_count)
    grad_proj_tiles = grad_proj_b.reshape(tile_count, tile_len, columns)

    def weight_step(running, tile_index):
        partial_value = lax.dot_general(normed_tiles[tile_index], grad_proj_tiles[tile_index], (((0,), (0,)), ((), ())), preferred_element_type=jnp.float32)
        return (running + bf16_round(partial_value), tile_index)
    grad_weight = lax.scan(weight_step, jnp.zeros((feature_count, columns), jnp.float32), jnp.arange(tile_count, dtype=jnp.int32))[0]
    grad_normed = lax.dot_general(grad_proj_b, w_bf, (((1,), (1,)), ((), ())), preferred_element_type=jnp.float32)
    grad_tokens = norm_backward(grad_normed, unit_rows, inverse, mod_scale).astype(jnp.bfloat16)
    return (attn_tiles.reshape(flat), grad_tokens, grad_weight.reshape(weight.shape))
```

```python
import functools
import math

import jax
import jax.numpy as jnp
from jax import lax
from jax.experimental import pallas as pl
from jax.experimental.pallas import tpu as pltpu
from jax.sharding import PartitionSpec as P

TT = 6
TH = 8
TW = 8
THETA = 256.0
EPS = 1e-06
F32 = jnp.float32
BF16 = jnp.bfloat16
LOG2E = 1.4426950408889634
LN2 = 0.6931471805599453
VMEM_LIMIT = 32 * 1024 * 1024

CHIPS = [(x, z, c) for x in range(4) for z in range(4) for c in range(2)]


def place(x, z, c):
    return (x * 4 + z) * 2 + c


def pairs_of(move):
    return [(place(*p), place(*move(*p))) for p in CHIPS]


CORE = pairs_of(lambda x, z, c: (x, z, 1 - c))
Z1 = pairs_of(lambda x, z, c: (x, z ^ 1, c))
Z3 = pairs_of(lambda x, z, c: (x, z ^ 3, c))
HALO = [
    (place(x, z, c), place(x - 1 if z < 2 else x + 1, z ^ 3, c))
    for x, z, c in CHIPS
    if 0 <= (x - 1 if z < 2 else x + 1) < 4
]


def move(value, pairs):
    return lax.ppermute(value, "dp", pairs)


def rope_tables(anchor, head_dim):
    token_ids = jnp.arange(TT * TH * TW, dtype=jnp.int32)[:, None]
    frames = anchor[0] + token_ids // (TH * TW)
    image_rows = anchor[1] + token_ids // TW % TH
    image_cols = anchor[2] + token_ids % TW
    section_t = head_dim // 8
    section_s = (head_dim - section_t) // 2
    channel = jnp.arange(head_dim, dtype=jnp.int32)[None, :]
    first = channel < section_t
    second = channel < section_t + section_s
    section_start = jnp.where(first, 0, jnp.where(second, section_t, section_t + section_s))
    section_len = jnp.where(first, section_t, section_s)
    pair_index = ((channel - section_start) // 2).astype(F32)
    frequency = THETA ** (-2.0 * pair_index / section_len.astype(F32))
    position = jnp.where(first, frames, jnp.where(second, image_rows, image_cols)).astype(F32)
    angles = position * frequency
    sine = jnp.sin(angles)
    even = channel % 2 == 0
    return (jnp.cos(angles), jnp.where(even, -sine, 0.0), jnp.where(even, 0.0, sine))


def normalize(tokens):
    floats = tokens.astype(F32)
    centred = floats - jnp.mean(floats, axis=-1, keepdims=True)
    inverse = lax.rsqrt(jnp.mean(centred * centred, axis=-1, keepdims=True) + EPS)
    return (centred * inverse, inverse)


def dot_nt(a, b):
    return lax.dot_general(a, b, (((1,), (1,)), ((), ())), preferred_element_type=F32)


def dot_tn(a, b):
    return lax.dot_general(a, b, (((0,), (0,)), ((), ())), preferred_element_type=F32)


def dot_nn(a, b):
    return jnp.dot(a, b, preferred_element_type=F32)


def turn(values, cosine, sine_up, sine_dn, sign):
    up = pltpu.roll(values, 127, 1)
    dn = pltpu.roll(values, 1, 1)
    return values * cosine + sign * (up * sine_up + dn * sine_dn)


def project_kernel(scale, normed, w, cos, sup, sdn, qg, kg, q_out, kv_out, raw_out):
    made = dot_nn(normed[...], w[...])
    c, su, sd = cos[...], sup[...], sdn[...]
    s0, s1, s2 = made[:, :128], made[:, 128:256], made[:, 256:]
    query = s0 * lax.rsqrt(jnp.mean(s0 * s0, axis=-1, keepdims=True) + EPS) * qg[...]
    key = s1 * lax.rsqrt(jnp.mean(s1 * s1, axis=-1, keepdims=True) + EPS) * kg[...]
    q_out[0] = (turn(query, c, su, sd, 1.0) * scale).astype(BF16)
    kv_out[0, 0] = turn(key, c, su, sd, 1.0).astype(BF16)
    kv_out[1, 0] = s2.astype(BF16)
    raw_out[0, 0] = s0
    raw_out[1, 0] = s1


def project(normed, w_whole, tables, q_gain, k_gain, heads, dim, scale):
    rows, width = normed.shape
    full = lambda shape: pl.BlockSpec(shape, lambda h: (0,) * len(shape))
    return pl.pallas_call(
        functools.partial(project_kernel, scale),
        grid=(heads,),
        in_specs=[
            full((rows, width)),
            pl.BlockSpec((width, 3 * dim), lambda h: (0, h)),
            full((rows, dim)),
            full((rows, dim)),
            full((rows, dim)),
            full((1, dim)),
            full((1, dim)),
        ],
        out_specs=[
            pl.BlockSpec((1, rows, dim), lambda h: (h, 0, 0)),
            pl.BlockSpec((2, 1, rows, dim), lambda h: (0, h, 0, 0)),
            pl.BlockSpec((2, 1, rows, dim), lambda h: (0, h, 0, 0)),
        ],
        out_shape=[
            jax.ShapeDtypeStruct((heads, rows, dim), BF16),
            jax.ShapeDtypeStruct((2, heads, rows, dim), BF16),
            jax.ShapeDtypeStruct((2, heads, rows, dim), F32),
        ],
        compiler_params=pltpu.CompilerParams(vmem_limit_bytes=VMEM_LIMIT),
        cost_estimate=pl.CostEstimate(
            flops=2 * rows * width * heads * 3 * dim, bytes_accessed=12_000_000, transcendentals=0
        ),
        name="project",
    )(normed, w_whole, *tables, q_gain[None, :], k_gain[None, :])


VMEM = pl.BlockSpec(memory_space=pltpu.VMEM)
SMEM = pl.BlockSpec(memory_space=pltpu.SMEM)


def forward_kernel(count, first, last, *refs):
    flags, q = refs[:2]
    tiles = refs[2 : 2 + count]
    rest = refs[2 + count :]
    heads, rows, dim = q.shape
    if first:
        acc = rest[0] if not last else None
    if first:
        acc[...] = jnp.zeros(acc.shape, F32)
    elif not last:
        before, acc = rest
        acc[...] = before[...]
    else:
        before, grad, attn_out, grad_ext, acc = rest
        acc[...] = before[...]
    ones = jnp.ones((rows, dim), BF16)
    for at, kv in enumerate(tiles):

        @pl.when(flags[at] != 0)
        def attend(kv=kv):
            for h in range(heads):
                weights = jnp.exp2(dot_nt(q[h], kv[0, h])).astype(BF16)
                acc[h] += dot_nn(weights, jnp.concatenate([kv[1, h], ones], axis=1))

    if last:
        lane = lax.broadcasted_iota(jnp.int32, (rows, dim), 1)
        for h in range(heads):
            share = 1.0 / acc[h, :, dim : dim + 1]
            attn = (acc[h, :, :dim] * share).astype(BF16)
            attn_out[:, h * dim : (h + 1) * dim] = attn
            g = grad[h].astype(F32)
            delta = jnp.sum(g * attn.astype(F32), axis=-1, keepdims=True) * share
            high = delta.astype(BF16).astype(F32)
            low = delta - high
            grad_ext[h, :, :dim] = (g * share).astype(BF16)
            grad_ext[h, :, dim:] = jnp.where(
                lane == 0, high, jnp.where(lane == 1, low, 0.0)
            ).astype(BF16)


def attend(flags, q, tiles, before=None, grad=None):
    heads, rows, dim = q.shape
    count = len(tiles)
    acc_shape = jax.ShapeDtypeStruct((heads, rows, 2 * dim), F32)
    last = grad is not None
    operands = [flags, q, *tiles]
    scratch = []
    if before is not None:
        operands.append(before)
    out_shape = [acc_shape]
    if last:
        operands.append(grad)
        out_shape = [
            jax.ShapeDtypeStruct((rows, heads * dim), BF16),
            jax.ShapeDtypeStruct((heads, rows, 2 * dim), BF16),
        ]
        scratch = [pltpu.VMEM(acc_shape.shape, F32)]
    return pl.pallas_call(
        functools.partial(forward_kernel, count, before is None, last),
        in_specs=[SMEM] + [VMEM] * (len(operands) - 1),
        out_specs=[VMEM] * len(out_shape),
        out_shape=out_shape,
        scratch_shapes=scratch,
        compiler_params=pltpu.CompilerParams(vmem_limit_bytes=VMEM_LIMIT),
        cost_estimate=pl.CostEstimate(
            flops=count * heads * 4 * rows * rows * dim,
            bytes_accessed=count * 600_000 + 2_000_000,
            transcendentals=count * heads * rows * rows,
        ),
        name="attend",
    )(*operands)


def backward_kernel(count, first, *refs):
    flags, q, grad_ext = refs[:3]
    tiles = refs[3 : 3 + count]
    rest = refs[3 + count :]
    heads, rows, dim = q.shape
    if first:
        dq, outs = rest[0], rest[1:]
        dq[...] = jnp.zeros(dq.shape, F32)
    else:
        before, dq, outs = rest[0], rest[1], rest[2:]
        dq[...] = before[...]
    lane = lax.broadcasted_iota(jnp.int32, (rows, dim), 1)
    minus = jnp.where(lane < 2, -1.0, 0.0).astype(BF16)
    for at, (kv, out) in enumerate(zip(tiles, outs)):

        @pl.when(flags[at] != 0)
        def differentiate(kv=kv, out=out):
            for h in range(heads):
                key = kv[0, h]
                exps = jnp.exp2(dot_nt(key, q[h]))
                inner = dot_nt(jnp.concatenate([kv[1, h], minus], axis=1), grad_ext[h])
                dscore = (exps * inner).astype(BF16)
                out[1, h] = dot_nn(exps.astype(BF16), grad_ext[h, :, :dim]).astype(BF16)
                out[0, h] = (dot_nn(dscore, q[h]) * LN2).astype(BF16)
                dq[h] += dot_tn(dscore, key)

        @pl.when(flags[at] == 0)
        def unused(out=out):
            out[...] = jnp.zeros(out.shape, BF16)


def differentiate(flags, q, grad_ext, tiles, before=None):
    heads, rows, dim = q.shape
    count = len(tiles)
    operands = [flags, q, grad_ext, *tiles]
    if before is not None:
        operands.append(before)
    result = pl.pallas_call(
        functools.partial(backward_kernel, count, before is None),
        in_specs=[SMEM] + [VMEM] * (len(operands) - 1),
        out_specs=[VMEM] * (1 + count),
        out_shape=[jax.ShapeDtypeStruct((heads, rows, dim), F32)]
        + [jax.ShapeDtypeStruct((2, heads, rows, dim), BF16)] * count,
        compiler_params=pltpu.CompilerParams(vmem_limit_bytes=VMEM_LIMIT),
        cost_estimate=pl.CostEstimate(
            flops=count * heads * 10 * rows * rows * dim,
            bytes_accessed=count * 1_200_000 + 2_000_000,
            transcendentals=count * heads * rows * rows,
        ),
        name="differentiate",
    )(*operands)
    return result[0], result[1:]


def pullback_kernel(scale, raw, dq, cos, sup, sdn, qg, kg, *refs):
    parts, out = refs[:-1], refs[-1]
    heads, rows, dim = dq.shape
    c, su, sd = cos[...], sup[...], sdn[...]

    def through_norm(grad, s, gain):
        grad = turn(grad, c, su, sd, -1.0) * gain
        inverse = lax.rsqrt(jnp.mean(s * s, axis=-1, keepdims=True) + EPS)
        along = jnp.mean(grad * s, axis=-1, keepdims=True) * (inverse * inverse)
        return inverse * (grad - s * along)

    for h in range(heads):
        key = parts[0][0, h].astype(F32)
        value = parts[0][1, h].astype(F32)
        for part in parts[1:]:
            key += part[0, h].astype(F32)
            value += part[1, h].astype(F32)
        base = 3 * dim * h
        out[:, base : base + dim] = through_norm(dq[h] * scale, raw[0, h], qg[...]).astype(BF16)
        out[:, base + dim : base + 2 * dim] = through_norm(key, raw[1, h], kg[...]).astype(BF16)
        out[:, base + 2 * dim : base + 3 * dim] = value.astype(BF16)


def pullback(raw, dq, tables, q_gain, k_gain, parts, scale):
    heads, rows, dim = dq.shape
    return pl.pallas_call(
        functools.partial(pullback_kernel, scale),
        in_specs=[VMEM] * (7 + len(parts)),
        out_specs=VMEM,
        out_shape=jax.ShapeDtypeStruct((rows, heads * 3 * dim), BF16),
        compiler_params=pltpu.CompilerParams(vmem_limit_bytes=VMEM_LIMIT),
        cost_estimate=pl.CostEstimate(flops=30_000_000, bytes_accessed=6_000_000, transcendentals=0),
        name="pullback",
    )(raw, dq, *tables, q_gain[None, :], k_gain[None, :], *parts)


def added(*parts):
    total = parts[0].astype(F32)
    for part in parts[1:]:
        total = total + part.astype(F32)
    return total.astype(BF16)


def local(tokens, tile_anchor, partners, weight, mod_shift, mod_scale, q_gain, k_gain, grad_out):
    rows = tokens.shape[0]
    heads, dim = weight.shape[1], weight.shape[3]
    columns = heads * 3 * dim
    score_scale = 1.0 / math.sqrt(dim)
    tile_total = lax.axis_size("dp")
    here = lax.axis_index("dp")
    slab, t, h = here // 4, here // 2 % 2, here % 2
    far = jnp.where(slab % 2 == 0, slab - 1, slab + 1)
    listed = partners[0]

    def flags_of(*spots):
        ids = jnp.stack([4 * s + 2 * (t ^ dt) + (h ^ dc) for s, dt, dc in spots])
        inside = jnp.logical_and(ids >= 0, ids < tile_total)
        return jnp.logical_and(
            inside, jnp.any(listed[None, :] == ids[:, None], axis=1)
        ).astype(jnp.int32)

    w_local = weight.reshape(weight.shape[0], columns).astype(BF16)
    w_whole = lax.all_gather(w_local, "dp", axis=0, tiled=True)

    unit_rows, inverse = normalize(tokens)
    normed = (unit_rows * (1.0 + mod_scale) + mod_shift).astype(BF16)
    tables = rope_tables(tile_anchor[0], dim)
    grad = grad_out.transpose(1, 0, 2)

    q, own, raw = project(
        normed, w_whole, tables, q_gain, k_gain, heads, dim, score_scale * LOG2E
    )

    near = move(own, Z3)
    side = move(own, Z1)
    edge = move(own, HALO)
    own_c = move(own, CORE)
    near1 = move(near, Z1)
    near_c = move(near, CORE)
    side_c = move(side, CORE)
    edge1 = move(edge, Z1)
    edge_c = move(edge, CORE)
    near1_c = move(near1, CORE)
    edge1_c = move(edge1, CORE)

    pal = slab ^ 1
    f_own = flags_of((slab, 0, 0), (slab, 0, 1))
    f_side = flags_of((slab, 1, 0), (slab, 1, 1))
    f_near = flags_of((pal, 1, 0), (pal, 1, 1))
    f_near1 = flags_of((pal, 0, 0), (pal, 0, 1))
    f_edge = flags_of((far, 1, 0), (far, 1, 1))
    f_edge1 = flags_of((far, 0, 0), (far, 0, 1))
    join = lambda *f: jnp.concatenate(f)

    (acc,) = attend(f_own, q, [own, own_c])
    (acc,) = attend(join(f_near, f_side), q, [near, near_c, side, side_c], acc)
    (acc,) = attend(join(f_edge, f_near1), q, [edge, edge_c, near1, near1_c], acc)
    attn_out, grad_ext = attend(f_edge1, q, [edge1, edge1_c], acc, grad)

    dq, (d_near1, d_near1_c) = differentiate(f_near1, q, grad_ext, [near1, near1_c])
    near1_back = move(added(d_near1, move(d_near1_c, CORE)), Z1)
    dq, (d_edge1, d_edge1_c) = differentiate(f_edge1, q, grad_ext, [edge1, edge1_c], dq)
    edge1_back = move(added(d_edge1, move(d_edge1_c, CORE)), Z1)
    dq, (d_near, d_near_c) = differentiate(f_near, q, grad_ext, [near, near_c], dq)
    near_back = move(added(d_near, move(d_near_c, CORE), near1_back), Z3)
    dq, (d_edge, d_edge_c) = differentiate(f_edge, q, grad_ext, [edge, edge_c], dq)
    edge_back = move(added(d_edge, move(d_edge_c, CORE), edge1_back), HALO)
    dq, (d_side, d_side_c) = differentiate(f_side, q, grad_ext, [side, side_c], dq)
    side_back = move(added(d_side, move(d_side_c, CORE)), Z1)
    dq, (d_own, d_own_c) = differentiate(f_own, q, grad_ext, [own, own_c], dq)
    own_back = move(d_own_c, CORE)

    grad_proj = pullback(
        raw,
        dq,
        tables,
        q_gain,
        k_gain,
        [d_own, own_back, side_back, near_back, edge_back],
        score_scale,
    )
    grad_part = dot_nt(grad_proj, w_whole)
    grad_share = lax.psum_scatter(
        grad_part.astype(BF16), "head", scatter_dimension=0, tiled=True
    ).astype(F32)
    grad_weight = (
        lax.psum_scatter(
            dot_tn(normed, grad_proj).astype(BF16), "dp", scatter_dimension=0, tiled=True
        )
        .astype(F32)
        .reshape(weight.shape)
    )
    share_rows = grad_share.shape[0]
    share_start = lax.axis_index("head") * share_rows
    unit, inverse = normalize(lax.dynamic_slice_in_dim(tokens, share_start, share_rows, 0))
    scaled = grad_share * (1.0 + mod_scale)
    centred = scaled - jnp.mean(scaled, axis=-1, keepdims=True)
    grad_tokens = inverse * (centred - unit * jnp.mean(scaled * unit, axis=-1, keepdims=True))
    return (attn_out.reshape(rows, heads, dim), grad_tokens.astype(BF16), grad_weight)


def solution(mesh):
    return jax.shard_map(
        local,
        mesh=mesh,
        in_specs=(
            P("dp", None),
            P("dp", None),
            P("dp", None),
            P("dp", "head", None, None),
            P(),
            P(),
            P(),
            P(),
            P("dp", "head", None),
        ),
        out_specs=(P("dp", "head", None), P(("dp", "head"), None), P("dp", "head", None, None)),
        check_vma=False,
    )
```

```python
import functools
import math

import jax
import jax.numpy as jnp
from jax import lax
from jax.experimental import pallas as pl
from jax.experimental.pallas import tpu as pltpu
from jax.sharding import PartitionSpec as P

TT = 6
TH = 8
TW = 8
THETA = 256.0
EPS = 1e-06
F32 = jnp.float32
QUICK = pl.CostEstimate(flops=1000, bytes_accessed=1000, transcendentals=0)
BF16 = jnp.bfloat16
LOG2E = 1.4426950408889634
LN2 = 0.6931471805599453
VMEM_LIMIT = 32 * 1024 * 1024
WIDE_LIMIT = 58 * 1024 * 1024

CHIPS = [(x, z, c) for x in range(4) for z in range(4) for c in range(2)]


def place(x, z, c):
    return (x * 4 + z) * 2 + c


def pairs_of(move):
    return [(place(*p), place(*move(*p))) for p in CHIPS]


CORE = pairs_of(lambda x, z, c: (x, z, 1 - c))
Z1 = pairs_of(lambda x, z, c: (x, z ^ 1, c))
Z3 = pairs_of(lambda x, z, c: (x, z ^ 3, c))
HALO = [
    (place(x, z, c), place(x - 1 if z < 2 else x + 1, z ^ 3, c))
    for x, z, c in CHIPS
    if 0 <= (x - 1 if z < 2 else x + 1) < 4
]
Z_RING = [pairs_of(lambda x, z, c, k=k: (x, (z + k) % 4, c)) for k in range(4)]
HEAD_UP = [(y, (y + 1) % 4) for y in range(4)]
HEAD_DOWN = [(y, (y + 3) % 4) for y in range(4)]
X_RING = [pairs_of(lambda x, z, c, k=k: ((x + k) % 4, z, c)) for k in range(4)]


def move(value, pairs):
    return lax.ppermute(value, "dp", pairs)


def rope_tables(anchor, head_dim):
    token_ids = jnp.arange(TT * TH * TW, dtype=jnp.int32)[:, None]
    frames = anchor[0] + token_ids // (TH * TW)
    image_rows = anchor[1] + token_ids // TW % TH
    image_cols = anchor[2] + token_ids % TW
    section_t = head_dim // 8
    section_s = (head_dim - section_t) // 2
    channel = jnp.arange(head_dim, dtype=jnp.int32)[None, :]
    first = channel < section_t
    second = channel < section_t + section_s
    section_start = jnp.where(first, 0, jnp.where(second, section_t, section_t + section_s))
    section_len = jnp.where(first, section_t, section_s)
    pair_index = ((channel - section_start) // 2).astype(F32)
    frequency = THETA ** (-2.0 * pair_index / section_len.astype(F32))
    position = jnp.where(first, frames, jnp.where(second, image_rows, image_cols)).astype(F32)
    angles = position * frequency
    sine = jnp.sin(angles)
    even = channel % 2 == 0
    return (jnp.cos(angles), jnp.where(even, -sine, 0.0), jnp.where(even, 0.0, sine))


def normalize(tokens):
    floats = tokens.astype(F32)
    centred = floats - jnp.mean(floats, axis=-1, keepdims=True)
    inverse = lax.rsqrt(jnp.mean(centred * centred, axis=-1, keepdims=True) + EPS)
    return centred * inverse


def dot_nt(a, b):
    return lax.dot_general(a, b, (((1,), (1,)), ((), ())), preferred_element_type=F32)


def dot_tn(a, b):
    return lax.dot_general(a, b, (((0,), (0,)), ((), ())), preferred_element_type=F32)


def dot_nn(a, b):
    return jnp.dot(a, b, preferred_element_type=F32)


def turn(values, cosine, sine_up, sine_dn, sign):
    up = pltpu.roll(values, 127, 1)
    dn = pltpu.roll(values, 1, 1)
    return values * cosine + sign * (up * sine_up + dn * sine_dn)


def project_kernel(scale, cut, normed, cos, sup, sdn, qg, kg, w, q_out, kv_out, raw_out, held, sems):
    width = w.shape[0]
    parts = 4
    copies = []
    for part in range(2):
        columns = slice(0, cut) if part == 0 else slice(cut, None)
        for at in range(parts):
            piece = (slice(at * width // parts, (at + 1) * width // parts), columns)
            copies.append(pltpu.make_async_copy(w.at[piece], held.at[piece], sems.at[part, at]))
    for copy in copies:
        copy.start()
    c, su, sd = cos[...], sup[...], sdn[...]
    for part in range(2):
        columns = slice(0, cut) if part == 0 else slice(cut, None)
        for copy in copies[parts * part : parts * (part + 1)]:
            copy.wait()
        made = dot_nn(normed[...], held[:, columns])
        for local_head in range(made.shape[1] // 384):
            h = local_head + part * cut // 384
            base = 384 * local_head
            s0, s1, s2 = (made[:, base + 128 * n : base + 128 * (n + 1)] for n in range(3))
            query = s0 * lax.rsqrt(jnp.mean(s0 * s0, axis=-1, keepdims=True) + EPS) * qg[...]
            key = s1 * lax.rsqrt(jnp.mean(s1 * s1, axis=-1, keepdims=True) + EPS) * kg[...]
            q_out[h] = (turn(query, c, su, sd, 1.0) * scale).astype(BF16)
            kv_out[0, h] = turn(key, c, su, sd, 1.0).astype(BF16)
            kv_out[1, h] = s2.astype(BF16)
            raw_out[0, h] = s0
            raw_out[1, h] = s1


def project(normed, w_whole, tables, q_gain, k_gain, heads, dim, scale):
    rows, width = normed.shape
    return pl.pallas_call(
        functools.partial(project_kernel, scale, 768),
        in_specs=[VMEM] * 6 + [pl.BlockSpec(memory_space=pl.ANY)],
        out_specs=[VMEM] * 3,
        out_shape=[
            jax.ShapeDtypeStruct((heads, rows, dim), BF16),
            jax.ShapeDtypeStruct((2, heads, rows, dim), BF16),
            jax.ShapeDtypeStruct((2, heads, rows, dim), F32),
        ],
        scratch_shapes=[
            pltpu.VMEM((width, heads * 3 * dim), BF16),
            pltpu.SemaphoreType.DMA((2, 4)),
        ],
        compiler_params=pltpu.CompilerParams(vmem_limit_bytes=WIDE_LIMIT),
        cost_estimate=QUICK,
        name="project",
    )(normed, *tables, q_gain[None, :], k_gain[None, :], w_whole)


VMEM = pl.BlockSpec(memory_space=pltpu.VMEM)
SMEM = pl.BlockSpec(memory_space=pltpu.SMEM)


def forward_kernel(count, first, last, *refs):
    flags, q = refs[:2]
    tiles = refs[2 : 2 + count]
    rest = refs[2 + count :]
    heads, rows, dim = q.shape
    if first:
        acc = rest[0] if not last else None
    if first:
        acc[...] = jnp.zeros(acc.shape, F32)
    elif not last:
        before, acc = rest
        acc[...] = before[...]
    else:
        before, grad, attn_out, grad_ext, acc = rest
        acc[...] = before[...]
    ones = jnp.ones((rows, dim), BF16)
    for at, kv in enumerate(tiles):

        @pl.when(flags[at] != 0)
        def attend(kv=kv):
            for h in range(heads):
                weights = jnp.exp2(dot_nt(q[h], kv[0, h])).astype(BF16)
                acc[h] += dot_nn(weights, jnp.concatenate([kv[1, h], ones], axis=1))

    if last:
        lane = lax.broadcasted_iota(jnp.int32, (rows, dim), 1)
        for h in range(heads):
            share = 1.0 / acc[h, :, dim : dim + 1]
            attn = (acc[h, :, :dim] * share).astype(BF16)
            attn_out[h] = attn
            g = grad[h].astype(F32)
            delta = jnp.sum(g * attn.astype(F32), axis=-1, keepdims=True) * share
            high = delta.astype(BF16).astype(F32)
            low = delta - high
            grad_ext[h, :, :dim] = (g * share).astype(BF16)
            grad_ext[h, :, dim:] = jnp.where(
                lane == 0, high, jnp.where(lane == 1, low, 0.0)
            ).astype(BF16)


def attend(flags, q, tiles, before=None, grad=None):
    heads, rows, dim = q.shape
    count = len(tiles)
    acc_shape = jax.ShapeDtypeStruct((heads, rows, 2 * dim), F32)
    last = grad is not None
    operands = [flags, q, *tiles]
    scratch = []
    if before is not None:
        operands.append(before)
    out_shape = [acc_shape]
    if last:
        operands.append(grad)
        out_shape = [
            jax.ShapeDtypeStruct((heads, rows, dim), BF16),
            jax.ShapeDtypeStruct((heads, rows, 2 * dim), BF16),
        ]
        scratch = [pltpu.VMEM(acc_shape.shape, F32)]
    return pl.pallas_call(
        functools.partial(forward_kernel, count, before is None, last),
        in_specs=[SMEM] + [VMEM] * (len(operands) - 1),
        out_specs=[VMEM] * len(out_shape),
        out_shape=out_shape,
        scratch_shapes=scratch,
        compiler_params=pltpu.CompilerParams(vmem_limit_bytes=VMEM_LIMIT),
        cost_estimate=QUICK,
        name="attend",
    )(*operands)


def backward_kernel(count, first, *refs):
    flags, q, grad_ext = refs[:3]
    tiles = refs[3 : 3 + count]
    rest = refs[3 + count :]
    heads, rows, dim = q.shape
    if first:
        dq, outs = rest[0], rest[1:]
        dq[...] = jnp.zeros(dq.shape, F32)
    else:
        before, dq, outs = rest[0], rest[1], rest[2:]
        dq[...] = before[...]
    lane = lax.broadcasted_iota(jnp.int32, (rows, dim), 1)
    minus = jnp.where(lane < 2, -1.0, 0.0).astype(BF16)
    for at, (kv, out) in enumerate(zip(tiles, outs)):

        @pl.when(flags[at] != 0)
        def differentiate(kv=kv, out=out):
            for h in range(heads):
                key = kv[0, h]
                exps = jnp.exp2(dot_nt(key, q[h]))
                inner = dot_nt(jnp.concatenate([kv[1, h], minus], axis=1), grad_ext[h])
                dscore = (exps * inner).astype(BF16)
                out[1, h] = dot_nn(exps.astype(BF16), grad_ext[h, :, :dim]).astype(BF16)
                out[0, h] = (dot_nn(dscore, q[h]) * LN2).astype(BF16)
                dq[h] += dot_tn(dscore, key)

        @pl.when(flags[at] == 0)
        def unused(out=out):
            out[...] = jnp.zeros(out.shape, BF16)


def differentiate(flags, q, grad_ext, tiles, before=None):
    heads, rows, dim = q.shape
    count = len(tiles)
    operands = [flags, q, grad_ext, *tiles]
    if before is not None:
        operands.append(before)
    result = pl.pallas_call(
        functools.partial(backward_kernel, count, before is None),
        in_specs=[SMEM] + [VMEM] * (len(operands) - 1),
        out_specs=[VMEM] * (1 + count),
        out_shape=[jax.ShapeDtypeStruct((heads, rows, dim), F32)]
        + [jax.ShapeDtypeStruct((2, heads, rows, dim), BF16)] * count,
        compiler_params=pltpu.CompilerParams(vmem_limit_bytes=VMEM_LIMIT),
        cost_estimate=QUICK,
        name="differentiate",
    )(*operands)
    return result[0], result[1:]


def pullback_kernel(scale, raw, dq, cos, sup, sdn, qg, kg, *refs):
    parts, out = refs[:-1], refs[-1]
    heads, rows, dim = dq.shape
    c, su, sd = cos[...], sup[...], sdn[...]

    def through_norm(grad, s, gain):
        grad = turn(grad, c, su, sd, -1.0) * gain
        inverse = lax.rsqrt(jnp.mean(s * s, axis=-1, keepdims=True) + EPS)
        along = jnp.mean(grad * s, axis=-1, keepdims=True) * (inverse * inverse)
        return inverse * (grad - s * along)

    for h in range(heads):
        key = parts[0][0, h].astype(F32)
        value = parts[0][1, h].astype(F32)
        for part in parts[1:]:
            key += part[0, h].astype(F32)
            value += part[1, h].astype(F32)
        base = 3 * dim * h
        out[:, base : base + dim] = through_norm(dq[h] * scale, raw[0, h], qg[...]).astype(BF16)
        out[:, base + dim : base + 2 * dim] = through_norm(key, raw[1, h], kg[...]).astype(BF16)
        out[:, base + 2 * dim : base + 3 * dim] = value.astype(BF16)


def pullback(raw, dq, tables, q_gain, k_gain, parts, scale):
    heads, rows, dim = dq.shape
    return pl.pallas_call(
        functools.partial(pullback_kernel, scale),
        in_specs=[VMEM] * (7 + len(parts)),
        out_specs=VMEM,
        out_shape=jax.ShapeDtypeStruct((rows, heads * 3 * dim), BF16),
        compiler_params=pltpu.CompilerParams(vmem_limit_bytes=VMEM_LIMIT),
        cost_estimate=QUICK,
        name="pullback",
    )(raw, dq, *tables, q_gain[None, :], k_gain[None, :], *parts)


def call(kernel, name, operands, shapes, smem=0, scratch=(), flops=1_000_000):
    return pl.pallas_call(
        kernel,
        in_specs=[SMEM] * smem + [VMEM] * (len(operands) - smem),
        out_specs=[VMEM] * len(shapes),
        out_shape=[jax.ShapeDtypeStruct(shape, kind) for shape, kind in shapes],
        scratch_shapes=list(scratch),
        compiler_params=pltpu.CompilerParams(vmem_limit_bytes=VMEM_LIMIT),
        cost_estimate=QUICK,
        name=name,
    )(*operands)


def weight_block(along_x, index, mine, other, grad, grad_other, cut):
    spot = (index, slice(None)) if along_x else (slice(None), index)
    rows = mine.shape[1] * mine.shape[2]
    left, right = mine[spot].reshape(rows, -1), other[spot].reshape(rows, -1)
    columns = slice(0, cut) if along_x else slice(cut, None)
    return dot_nn(left, grad[:, columns]) + dot_nn(right, grad_other[:, columns])


def weigh_far_kernel(cut, spot, mine, other, grad, grad_other, *outs):
    for axis in range(2):
        block = weight_block(axis == 0, (spot[axis] + 2) % 4, mine, other, grad, grad_other, cut)
        half = block.shape[0] // 2
        outs[2 * axis][...] = block[:half].astype(BF16)
        outs[2 * axis + 1][...] = block[half:].astype(BF16)


def weigh_near_kernel(cut, spot, mine, other, grad, grad_other, *outs):
    for axis in range(2):
        for at, step in enumerate((1, 3, 0)):
            out = outs[3 * axis + at]
            out[...] = weight_block(
                axis == 0, (spot[axis] + step) % 4, mine, other, grad, grad_other, cut
            ).astype(out.dtype)


def merge_kernel(*refs):
    count = len(refs) // 3
    blocks, came, outs = refs[:count], refs[count : 2 * count], refs[2 * count :]
    for at in range(count):
        block, extra, out = blocks[at], came[at], outs[at]
        half = extra.shape[0]
        total = (block[pl.ds(half * (at % 2), half)].astype(F32) + extra[...].astype(F32)).astype(
            BF16
        )
        keep = pl.ds(half * (1 - at % 2), half)
        out[pl.ds(half * (at % 2), half)] = total
        out[keep] = block[keep]


def spread_kernel(spot, own_x, fore_x, back_x, own_z, fore_z, back_z, *refs):
    outs, sums = refs[:8], refs[8:]
    for axis, parts in enumerate(((own_x, fore_x, back_x), (own_z, fore_z, back_z))):
        total = parts[0][...] + parts[1][...].astype(F32) + parts[2][...].astype(F32)
        sums[axis][...] = total.reshape(sums[axis].shape)
        for step in range(4):
            out = outs[4 * axis + step]
            out[...] = sums[axis][(spot[1 - axis] + step) % 4].astype(out.dtype)


def settle_kernel(cut, *refs):
    parts, out = refs[:-1], refs[-1]
    for axis in range(2):
        total = parts[4 * axis][...]
        for part in parts[4 * axis + 1 : 4 * axis + 4]:
            total = total + part[...].astype(F32)
        first = axis * cut // 128
        for at in range(total.shape[1] // 128):
            out[(first + at) // 3, (first + at) % 3] = total[:, at * 128 : (at + 1) * 128]


def pack_kernel(weight, out):
    for at in range(9):
        out[:, at * 128 : (at + 1) * 128] = weight[at // 3, at % 3].astype(BF16)


def input_grad_kernel(spot, grad, w, far_a, far_b, fore, back, own, turned, held, sems):
    share = own.shape[0]
    parts = sems.shape[0]
    chunk = w.shape[0] // parts
    copies = []
    for at in range(parts):
        piece = slice(at * chunk, (at + 1) * chunk)
        copies.append(pltpu.make_async_copy(w.at[piece], held.at[piece], sems.at[at]))
    for copy in copies:
        copy.start()
    for at, step in enumerate((2, 1, 3, 0)):
        start = pl.multiple_of((spot[2] + step) % 4 * share, share)
        turned[pl.ds(at * share, share)] = grad[pl.ds(start, share)]
    half = share // 2
    for at in range(parts):
        piece = slice(at * chunk, (at + 1) * chunk)
        copies[at].wait()
        made = dot_nt(turned[...], held[piece])
        far_a[:, piece] = made[:half].astype(BF16)
        far_b[:, piece] = made[half:share].astype(BF16)
        fore[:, piece] = made[share : 2 * share].astype(BF16)
        back[:, piece] = made[2 * share : 3 * share].astype(BF16)
        own[:, piece] = made[3 * share :]


def input_grad(spot, grad, w_whole):
    rows, columns = grad.shape
    width = w_whole.shape[0]
    share, parts = rows // 4, 6
    heights = (share // 2, share // 2, share, share, share)
    kinds = (BF16, BF16, BF16, BF16, F32)
    return pl.pallas_call(
        input_grad_kernel,
        in_specs=[SMEM, VMEM, pl.BlockSpec(memory_space=pl.ANY)],
        out_specs=[VMEM] * 5,
        out_shape=[jax.ShapeDtypeStruct((n, width), kind) for n, kind in zip(heights, kinds)],
        scratch_shapes=[
            pltpu.VMEM((rows, columns), BF16),
            pltpu.VMEM((width, columns), BF16),
            pltpu.SemaphoreType.DMA((parts,)),
        ],
        compiler_params=pltpu.CompilerParams(vmem_limit_bytes=WIDE_LIMIT),
        cost_estimate=QUICK,
        name="input_grad",
    )(spot, grad, w_whole)


def finish_kernel(own, fore, back, tokens, mod_scale, out):
    floats = tokens[...].astype(F32)
    centred = floats - jnp.mean(floats, axis=-1, keepdims=True)
    inverse = lax.rsqrt(jnp.mean(centred * centred, axis=-1, keepdims=True) + EPS)
    unit = centred * inverse
    total = own[...] + fore[...].astype(F32) + back[...].astype(F32)
    scaled = total * (1.0 + mod_scale[...])
    inner = scaled - jnp.mean(scaled, axis=-1, keepdims=True)
    along = jnp.mean(scaled * unit, axis=-1, keepdims=True)
    out[...] = (inverse * (inner - unit * along)).astype(BF16)


def after(*values):
    return lax.optimization_barrier(values)


def added(*parts):
    total = parts[0].astype(F32)
    for part in parts[1:]:
        total = total + part.astype(F32)
    return total.astype(BF16)


def local(tokens, tile_anchor, partners, weight, mod_shift, mod_scale, q_gain, k_gain, grad_out):
    rows = tokens.shape[0]
    heads, dim = weight.shape[1], weight.shape[3]
    columns = heads * 3 * dim
    score_scale = 1.0 / math.sqrt(dim)
    tile_total = lax.axis_size("dp")
    here = lax.axis_index("dp")
    slab, t, h = here // 4, here // 2 % 2, here % 2
    far = jnp.where(slab % 2 == 0, slab - 1, slab + 1)
    listed = partners[0]

    def flags_of(*spots):
        ids = jnp.stack([4 * s + 2 * (t ^ dt) + (h ^ dc) for s, dt, dc in spots])
        inside = jnp.logical_and(ids >= 0, ids < tile_total)
        return jnp.logical_and(
            inside, jnp.any(listed[None, :] == ids[:, None], axis=1)
        ).astype(jnp.int32)

    (w_local,) = call(
        pack_kernel, "pack", [weight.transpose(1, 2, 0, 3)], [((weight.shape[0], columns), BF16)]
    )
    w_whole = lax.all_gather(w_local, "dp", axis=0, tiled=True)

    unit_rows = normalize(tokens)
    normed = (unit_rows * (1.0 + mod_scale) + mod_shift).astype(BF16)
    tables = rope_tables(tile_anchor[0], dim)
    head_at = lax.axis_index("head")
    spot = jnp.stack([here // 8, here // 2 % 4, head_at]).astype(jnp.int32)
    tokens_share = lax.dynamic_slice_in_dim(tokens, head_at * (rows // 4), rows // 4, 0)
    by_owner = normed.T.reshape(4, 4, 2, weight.shape[0], rows)
    mine = lax.dynamic_index_in_dim(by_owner, h, 2, keepdims=False)
    other = move(lax.dynamic_index_in_dim(by_owner, 1 - h, 2, keepdims=False), CORE)
    grad = grad_out.transpose(1, 0, 2)
    normed, mine, other, grad, tokens_share, *tables = after(
        normed, mine, other, grad, tokens_share, *tables
    )

    q, own, raw = project(
        normed, w_whole, tables, q_gain, k_gain, heads, dim, score_scale * LOG2E
    )

    pal = slab ^ 1
    f_own = flags_of((slab, 0, 0), (slab, 0, 1))
    f_side = flags_of((slab, 1, 0), (slab, 1, 1))
    f_near = flags_of((pal, 1, 0), (pal, 1, 1))
    f_near1 = flags_of((pal, 0, 0), (pal, 0, 1))
    f_edge = flags_of((far, 1, 0), (far, 1, 1))
    f_edge1 = flags_of((far, 0, 0), (far, 0, 1))
    join = lambda *f: jnp.concatenate(f)

    near = move(own, Z3)
    side = move(own, Z1)
    own_c = move(own, CORE)
    (acc,) = attend(f_own, q, [own, own_c])
    near, acc, own_then = after(near, acc, own)
    edge = move(own_then, HALO)
    near1 = move(near, Z1)
    near_c = move(near, CORE)
    side_c = move(side, CORE)
    (acc,) = attend(join(f_near, f_side), q, [near, near_c, side, side_c], acc)
    edge, acc = after(edge, acc)
    edge1 = move(edge, Z1)
    edge_c = move(edge, CORE)
    near1_c = move(near1, CORE)
    (acc,) = attend(join(f_edge, f_near1), q, [edge, edge_c, near1, near1_c], acc)
    edge1, acc = after(edge1, acc)
    edge1_c = move(edge1, CORE)
    attn_out, grad_ext = attend(f_edge1, q, [edge1, edge1_c], acc, grad)

    dq, (d_near1, d_near1_c) = differentiate(f_near1, q, grad_ext, [near1, near1_c])
    near1_swap = move(d_near1_c, CORE)
    dq, (d_edge1, d_edge1_c) = differentiate(f_edge1, q, grad_ext, [edge1, edge1_c], dq)
    edge1_swap = move(d_edge1_c, CORE)
    near1_sum = added(d_near1, near1_swap)
    near1_back = move(near1_sum, Z1)
    near1_sum, dq = after(near1_sum, dq)
    dq, (d_near, d_near_c) = differentiate(f_near, q, grad_ext, [near, near_c], dq)
    near_swap = move(d_near_c, CORE)
    edge1_sum = added(d_edge1, edge1_swap)
    edge1_back = move(edge1_sum, Z1)
    edge1_sum, dq = after(edge1_sum, dq)
    dq, (d_edge, d_edge_c) = differentiate(f_edge, q, grad_ext, [edge, edge_c], dq)
    edge_swap = move(d_edge_c, CORE)
    near_sum = added(d_near, near_swap, near1_back)
    near_back = move(near_sum, Z3)
    near_sum, dq = after(near_sum, dq)
    dq, (d_side, d_side_c) = differentiate(f_side, q, grad_ext, [side, side_c], dq)
    side_swap = move(d_side_c, CORE)
    edge_sum = added(d_edge, edge_swap, edge1_back)
    edge_back = move(edge_sum, HALO)
    side_sum = added(d_side, side_swap)
    side_back = move(side_sum, Z1)
    edge_sum, side_sum, dq = after(edge_sum, side_sum, dq)
    dq, (d_own, d_own_c) = differentiate(f_own, q, grad_ext, [own, own_c], dq)
    own_back = move(d_own_c, CORE)

    grad_proj = pullback(
        raw,
        dq,
        tables,
        q_gain,
        k_gain,
        [d_own, own_back, side_back, near_back, edge_back],
        score_scale,
    )
    grad_proj_other = move(grad_proj, CORE)
    far_a, far_b, fore, back, own_rows = input_grad(spot, grad_proj, w_whole)
    came_a = lax.ppermute(far_a, "head", HEAD_UP)
    came_b = lax.ppermute(far_b, "head", HEAD_DOWN)
    grad_proj_other, own_rows = after(grad_proj_other, own_rows)
    width = weight.shape[0]
    cut = 640
    rest = columns - cut
    lhs = [spot, mine, other, grad_proj, grad_proj_other]
    flops = 2 * rows * 2 * width * 16 * columns // 4
    far = call(
        functools.partial(weigh_far_kernel, cut),
        "weigh_far",
        lhs,
        [((2 * width, cut), BF16)] * 2 + [((2 * width, rest), BF16)] * 2,
        smem=1,
        flops=flops,
    )
    came = [
        move(far[0], X_RING[1]),
        move(far[1], X_RING[3]),
        move(far[2], Z_RING[1]),
        move(far[3], Z_RING[3]),
    ]
    near_blocks = call(
        functools.partial(weigh_near_kernel, cut),
        "weigh_near",
        lhs,
        [((4 * width, n), kind) for n in (cut, rest) for kind in (BF16, BF16, F32)],
        smem=1,
        flops=3 * flops,
    )
    blocks = [near_blocks[0], near_blocks[1], near_blocks[3], near_blocks[4]]
    came_a, *blocks = after(came_a, *blocks)
    fore_sum, back_sum = call(
        merge_kernel,
        "merge_rows",
        [fore, back, came_a, came_b],
        [(fore.shape, BF16)] * 2,
    )
    fore_got = lax.ppermute(fore_sum, "head", HEAD_UP)
    back_got = lax.ppermute(back_sum, "head", HEAD_DOWN)
    fore_sum, *blocks = after(fore_sum, *blocks)
    sums = call(merge_kernel, "merge_weight", blocks + came, [(b.shape, BF16) for b in blocks])
    got = [
        move(sums[0], X_RING[1]),
        move(sums[1], X_RING[3]),
        move(sums[2], Z_RING[1]),
        move(sums[3], Z_RING[3]),
    ]
    own_x, own_z = near_blocks[2], near_blocks[5]
    pieces = call(
        spread_kernel,
        "spread",
        [spot, own_x, got[0], got[1], own_z, got[2], got[3]],
        [((width, n), F32 if step == 0 else BF16) for n in (cut, rest) for step in range(4)],
        smem=1,
        scratch=[pltpu.VMEM((4, width, cut), F32), pltpu.VMEM((4, width, rest), F32)],
    )
    last = []
    for axis, ring in enumerate((Z_RING, X_RING)):
        last.append(pieces[4 * axis])
        last += [move(pieces[4 * axis + step], ring[step]) for step in (1, 2, 3)]
    (grad_tokens,) = call(
        finish_kernel,
        "finish",
        [own_rows, fore_got, back_got, tokens_share, mod_scale[None, :]],
        [(tokens_share.shape, BF16)],
    )
    (grad_weight,) = call(
        functools.partial(settle_kernel, cut), "settle", last, [((heads, 3, width, dim), F32)]
    )
    return (
        attn_out.transpose(1, 0, 2),
        grad_tokens,
        grad_weight.transpose(2, 0, 1, 3),
    )


def solution(mesh):
    return jax.shard_map(
        local,
        mesh=mesh,
        in_specs=(
            P("dp", None),
            P("dp", None),
            P("dp", None),
            P("dp", "head", None, None),
            P(),
            P(),
            P(),
            P(),
            P("dp", "head", None),
        ),
        out_specs=(P("dp", "head", None), P(("dp", "head"), None), P("dp", "head", None, None)),
        check_vma=False,
    )
```

```python
import functools
import math

import jax
import jax.numpy as jnp
from jax import lax
from jax.experimental import pallas as pl
from jax.experimental.pallas import tpu as pltpu
from jax.sharding import PartitionSpec as P

TT = 6
TH = 8
TW = 8
THETA = 256.0
EPS = 1e-06
F32 = jnp.float32
LONG = pl.CostEstimate(flops=20_000_000_000, bytes_accessed=30_000_000, transcendentals=0)
QUICK = pl.CostEstimate(flops=1000, bytes_accessed=1000, transcendentals=0)
BF16 = jnp.bfloat16
LOG2E = 1.4426950408889634
LN2 = 0.6931471805599453
VMEM_LIMIT = 32 * 1024 * 1024
WIDE_LIMIT = 58 * 1024 * 1024

CHIPS = [(x, z, c) for x in range(4) for z in range(4) for c in range(2)]


def place(x, z, c):
    return (x * 4 + z) * 2 + c


def pairs_of(move):
    return [(place(*p), place(*move(*p))) for p in CHIPS]


CORE = pairs_of(lambda x, z, c: (x, z, 1 - c))
Z1 = pairs_of(lambda x, z, c: (x, z ^ 1, c))
Z3 = pairs_of(lambda x, z, c: (x, z ^ 3, c))
HALO = [
    (place(x, z, c), place(x - 1 if z < 2 else x + 1, z ^ 3, c))
    for x, z, c in CHIPS
    if 0 <= (x - 1 if z < 2 else x + 1) < 4
]
Z_RING = [pairs_of(lambda x, z, c, k=k: (x, (z + k) % 4, c)) for k in range(4)]
ORDERS = (((4, 1, 12, 3), (12, 3, 4, 1)), ((1, 12, 3, 4), (3, 4, 1, 12)))
HEAD_ORDERS = ((1, 3), (3, 1))


def exchange(value, stream, step):
    return lax.ppermute(
        value,
        "dp",
        [
            (chip * 2 + c, (chip ^ ORDERS[stream][c][step]) * 2 + c)
            for chip in range(16)
            for c in range(2)
        ],
    )


def head_exchange(value, step):
    return lax.ppermute(
        value,
        ("dp", "head"),
        [
            (device * 4 + y, device * 4 + (y ^ HEAD_ORDERS[device % 2][step]))
            for device in range(32)
            for y in range(4)
        ],
    )


def reach(start, masks, core):
    steps = len(masks[0])
    table = []
    for c in range(2):
        row = []
        for at in range(2**steps):
            mask = 0
            for step in range(steps):
                if at >> (steps - 1 - step) & 1:
                    mask ^= masks[c][step]
            row.append(mask)
        table.append(row)
    return start ^ jnp.where(core == 0, jnp.array(table[0]), jnp.array(table[1])).astype(jnp.int32)


ACROSS = pairs_of(lambda x, z, c: (x, z ^ (3 if c else 1), c))


def move(value, pairs):
    return lax.ppermute(value, "dp", pairs)


def rope_tables(anchor, head_dim):
    token_ids = jnp.arange(TT * TH * TW, dtype=jnp.int32)[:, None]
    frames = anchor[0] + token_ids // (TH * TW)
    image_rows = anchor[1] + token_ids // TW % TH
    image_cols = anchor[2] + token_ids % TW
    section_t = head_dim // 8
    section_s = (head_dim - section_t) // 2
    channel = jnp.arange(head_dim, dtype=jnp.int32)[None, :]
    first = channel < section_t
    second = channel < section_t + section_s
    section_start = jnp.where(first, 0, jnp.where(second, section_t, section_t + section_s))
    section_len = jnp.where(first, section_t, section_s)
    pair_index = ((channel - section_start) // 2).astype(F32)
    frequency = THETA ** (-2.0 * pair_index / section_len.astype(F32))
    position = jnp.where(first, frames, jnp.where(second, image_rows, image_cols)).astype(F32)
    angles = position * frequency
    sine = jnp.sin(angles)
    even = channel % 2 == 0
    return (jnp.cos(angles), jnp.where(even, -sine, 0.0), jnp.where(even, 0.0, sine))


def normalize(tokens):
    floats = tokens.astype(F32)
    centred = floats - jnp.mean(floats, axis=-1, keepdims=True)
    inverse = lax.rsqrt(jnp.mean(centred * centred, axis=-1, keepdims=True) + EPS)
    return centred * inverse


def dot_nt(a, b):
    return lax.dot_general(a, b, (((1,), (1,)), ((), ())), preferred_element_type=F32)


def dot_tn(a, b):
    return lax.dot_general(a, b, (((0,), (0,)), ((), ())), preferred_element_type=F32)


def dot_nn(a, b):
    return jnp.dot(a, b, preferred_element_type=F32)


def turn(values, cosine, sine_up, sine_dn, sign):
    up = pltpu.roll(values, 127, 1)
    dn = pltpu.roll(values, 1, 1)
    return values * cosine + sign * (up * sine_up + dn * sine_dn)


def project_kernel(scale, cut, normed, cos, sup, sdn, qg, kg, w, q_out, kv_out, raw_out, held, sems):
    width = w.shape[0]
    parts = 4
    copies = []
    for part in range(2):
        columns = slice(0, cut) if part == 0 else slice(cut, None)
        for at in range(parts):
            piece = (slice(at * width // parts, (at + 1) * width // parts), columns)
            copies.append(pltpu.make_async_copy(w.at[piece], held.at[piece], sems.at[part, at]))
    for copy in copies[:parts]:
        copy.start()
    c, su, sd = cos[...], sup[...], sdn[...]
    for part in range(2):
        columns = slice(0, cut) if part == 0 else slice(cut, None)
        for copy in copies[parts * part : parts * (part + 1)]:
            copy.wait()
        if part == 0:
            for copy in copies[parts:]:
                copy.start()
        made = dot_nn(normed[...], held[:, columns])
        for local_head in range(made.shape[1] // 384):
            h = local_head + part * cut // 384
            base = 384 * local_head
            s0, s1, s2 = (made[:, base + 128 * n : base + 128 * (n + 1)] for n in range(3))
            query = s0 * lax.rsqrt(jnp.mean(s0 * s0, axis=-1, keepdims=True) + EPS) * qg[...]
            key = s1 * lax.rsqrt(jnp.mean(s1 * s1, axis=-1, keepdims=True) + EPS) * kg[...]
            q_out[h] = (turn(query, c, su, sd, 1.0) * scale).astype(BF16)
            kv_out[0, h] = turn(key, c, su, sd, 1.0).astype(BF16)
            kv_out[1, h] = s2.astype(BF16)
            raw_out[0, h] = s0
            raw_out[1, h] = s1


def project(normed, w_whole, tables, q_gain, k_gain, heads, dim, scale):
    rows, width = normed.shape
    return pl.pallas_call(
        functools.partial(project_kernel, scale, 384),
        in_specs=[VMEM] * 6 + [pl.BlockSpec(memory_space=pl.ANY)],
        out_specs=[VMEM] * 3,
        out_shape=[
            jax.ShapeDtypeStruct((heads, rows, dim), BF16),
            jax.ShapeDtypeStruct((2, heads, rows, dim), BF16),
            jax.ShapeDtypeStruct((2, heads, rows, dim), F32),
        ],
        scratch_shapes=[
            pltpu.VMEM((width, heads * 3 * dim), BF16),
            pltpu.SemaphoreType.DMA((2, 4)),
        ],
        compiler_params=pltpu.CompilerParams(vmem_limit_bytes=WIDE_LIMIT),
        cost_estimate=QUICK,
        name="project",
    )(normed, *tables, q_gain[None, :], k_gain[None, :], w_whole)


VMEM = pl.BlockSpec(memory_space=pltpu.VMEM)
SMEM = pl.BlockSpec(memory_space=pltpu.SMEM)


def forward_kernel(count, first, last, *refs):
    flags, q = refs[:2]
    tiles = refs[2 : 2 + count]
    rest = refs[2 + count :]
    heads, rows, dim = q.shape
    if first:
        acc = rest[0] if not last else None
    if first:
        acc[...] = jnp.zeros(acc.shape, F32)
    elif not last:
        before, acc = rest
        acc[...] = before[...]
    else:
        before, grad, attn_out, grad_ext, acc = rest
        acc[...] = before[...]
    ones = jnp.ones((rows, dim), BF16)
    for at, kv in enumerate(tiles):

        @pl.when(flags[at] != 0)
        def attend(kv=kv):
            for h in range(heads):
                weights = jnp.exp2(dot_nt(q[h], kv[0, h])).astype(BF16)
                acc[h] += dot_nn(weights, jnp.concatenate([kv[1, h], ones], axis=1))

    if last:
        lane = lax.broadcasted_iota(jnp.int32, (rows, dim), 1)
        for h in range(heads):
            share = 1.0 / acc[h, :, dim : dim + 1]
            attn = (acc[h, :, :dim] * share).astype(BF16)
            attn_out[h] = attn
            g = grad[h].astype(F32)
            delta = jnp.sum(g * attn.astype(F32), axis=-1, keepdims=True) * share
            high = delta.astype(BF16).astype(F32)
            low = delta - high
            grad_ext[h, :, :dim] = (g * share).astype(BF16)
            grad_ext[h, :, dim:] = jnp.where(
                lane == 0, high, jnp.where(lane == 1, low, 0.0)
            ).astype(BF16)


def attend(flags, q, tiles, before=None, grad=None):
    heads, rows, dim = q.shape
    count = len(tiles)
    acc_shape = jax.ShapeDtypeStruct((heads, rows, 2 * dim), F32)
    last = grad is not None
    operands = [flags, q, *tiles]
    scratch = []
    if before is not None:
        operands.append(before)
    out_shape = [acc_shape]
    if last:
        operands.append(grad)
        out_shape = [
            jax.ShapeDtypeStruct((heads, rows, dim), BF16),
            jax.ShapeDtypeStruct((heads, rows, 2 * dim), BF16),
        ]
        scratch = [pltpu.VMEM(acc_shape.shape, F32)]
    return pl.pallas_call(
        functools.partial(forward_kernel, count, before is None, last),
        in_specs=[SMEM] + [VMEM] * (len(operands) - 1),
        out_specs=[VMEM] * len(out_shape),
        out_shape=out_shape,
        scratch_shapes=scratch,
        compiler_params=pltpu.CompilerParams(vmem_limit_bytes=VMEM_LIMIT),
        cost_estimate=QUICK,
        name="attend",
    )(*operands)


def backward_kernel(count, first, *refs):
    flags, q, grad_ext = refs[:3]
    tiles = refs[3 : 3 + count]
    rest = refs[3 + count :]
    heads, rows, dim = q.shape
    if first:
        dq, outs = rest[0], rest[1:]
        dq[...] = jnp.zeros(dq.shape, F32)
    else:
        before, dq, outs = rest[0], rest[1], rest[2:]
        dq[...] = before[...]
    lane = lax.broadcasted_iota(jnp.int32, (rows, dim), 1)
    minus = jnp.where(lane < 2, -1.0, 0.0).astype(BF16)
    for at, (kv, out) in enumerate(zip(tiles, outs)):

        @pl.when(flags[at] != 0)
        def differentiate(kv=kv, out=out):
            for h in range(heads):
                key = kv[0, h]
                exps = jnp.exp2(dot_nt(key, q[h]))
                inner = dot_nt(jnp.concatenate([kv[1, h], minus], axis=1), grad_ext[h])
                dscore = (exps * inner).astype(BF16)
                out[1, h] = dot_nn(exps.astype(BF16), grad_ext[h, :, :dim]).astype(BF16)
                out[0, h] = (dot_nn(dscore, q[h]) * LN2).astype(BF16)
                dq[h] += dot_tn(dscore, key)

        @pl.when(flags[at] == 0)
        def unused(out=out):
            out[...] = jnp.zeros(out.shape, BF16)


def differentiate(flags, q, grad_ext, tiles, before=None, cost=QUICK):
    heads, rows, dim = q.shape
    count = len(tiles)
    operands = [flags, q, grad_ext, *tiles]
    if before is not None:
        operands.append(before)
    result = pl.pallas_call(
        functools.partial(backward_kernel, count, before is None),
        in_specs=[SMEM] + [VMEM] * (len(operands) - 1),
        out_specs=[VMEM] * (1 + count),
        out_shape=[jax.ShapeDtypeStruct((heads, rows, dim), F32)]
        + [jax.ShapeDtypeStruct((2, heads, rows, dim), BF16)] * count,
        compiler_params=pltpu.CompilerParams(vmem_limit_bytes=VMEM_LIMIT),
        cost_estimate=cost,
        name="differentiate",
    )(*operands)
    return result[0], result[1:]


def pullback_kernel(scale, raw, dq, cos, sup, sdn, qg, kg, *refs):
    parts, out = refs[:-1], refs[-1]
    heads, rows, dim = dq.shape
    c, su, sd = cos[...], sup[...], sdn[...]

    def through_norm(grad, s, gain):
        grad = turn(grad, c, su, sd, -1.0) * gain
        inverse = lax.rsqrt(jnp.mean(s * s, axis=-1, keepdims=True) + EPS)
        along = jnp.mean(grad * s, axis=-1, keepdims=True) * (inverse * inverse)
        return inverse * (grad - s * along)

    for h in range(heads):
        key = parts[0][0, h].astype(F32)
        value = parts[0][1, h].astype(F32)
        for part in parts[1:]:
            key += part[0, h].astype(F32)
            value += part[1, h].astype(F32)
        base = 3 * dim * h
        out[:, base : base + dim] = through_norm(dq[h] * scale, raw[0, h], qg[...]).astype(BF16)
        out[:, base + dim : base + 2 * dim] = through_norm(key, raw[1, h], kg[...]).astype(BF16)
        out[:, base + 2 * dim : base + 3 * dim] = value.astype(BF16)


def pullback(raw, dq, tables, q_gain, k_gain, parts, scale):
    heads, rows, dim = dq.shape
    return pl.pallas_call(
        functools.partial(pullback_kernel, scale),
        in_specs=[VMEM] * (7 + len(parts)),
        out_specs=VMEM,
        out_shape=jax.ShapeDtypeStruct((rows, heads * 3 * dim), BF16),
        compiler_params=pltpu.CompilerParams(vmem_limit_bytes=VMEM_LIMIT),
        cost_estimate=QUICK,
        name="pullback",
    )(raw, dq, *tables, q_gain[None, :], k_gain[None, :], *parts)


def call(kernel, name, operands, shapes, smem=0, scratch=(), flops=1_000_000):
    return pl.pallas_call(
        kernel,
        in_specs=[SMEM] * smem + [VMEM] * (len(operands) - smem),
        out_specs=[VMEM] * len(shapes),
        out_shape=[jax.ShapeDtypeStruct(shape, kind) for shape, kind in shapes],
        scratch_shapes=list(scratch),
        compiler_params=pltpu.CompilerParams(vmem_limit_bytes=VMEM_LIMIT),
        cost_estimate=QUICK,
        name=name,
    )(*operands)


def weigh_kernel(first, order, mine, other, grad, grad_other, *outs):
    half = mine.shape[1] // 2
    for stream, out in enumerate(outs):
        rows = pl.ds(stream * half, half)
        chips = [order[16 * stream + first + at] for at in range(8)]
        left = jnp.concatenate([mine[chip, rows] for chip in chips], axis=0)
        right = jnp.concatenate([other[chip, rows] for chip in chips], axis=0)
        made = dot_nn(left, grad[...]) + dot_nn(right, grad_other[...])
        out[...] = made.astype(out.dtype)


def halve_kernel(*refs):
    for stream in range(2):
        held, came, sent, kept = (refs[2 * n + stream] for n in range(4))
        half = sent.shape[0]
        low, high = pl.ds(0, half), pl.ds(half, half)
        sent[...] = (held[high] + came[high].astype(F32)).astype(BF16)
        kept[...] = held[low] + came[low].astype(F32)


def settle_kernel(held_a, held_b, came_a, came_b, out):
    for stream, (held, came) in enumerate(((held_a, came_a), (held_b, came_b))):
        total = held[...] + came[...].astype(F32)
        half = total.shape[0]
        for at in range(9):
            out[at // 3, at % 3, pl.ds(stream * half, half)] = total[:, at * 128 : (at + 1) * 128]


def merge_kernel(held, came, out):
    share = out.shape[0]
    out[...] = (held[pl.ds(share, share)] + came[pl.ds(share, share)].astype(F32)).astype(BF16)


def pack_kernel(weight, out):
    for at in range(9):
        out[:, at * 128 : (at + 1) * 128] = weight[at // 3, at % 3].astype(BF16)


def input_grad_kernel(order, grad, w, sent, held, turned, stored, sems):
    share = grad.shape[0] // 4
    parts = sems.shape[0]
    chunk = w.shape[0] // parts
    ahead = 2

    def piece(at):
        return slice(at * chunk, (at + 1) * chunk)

    copies = [
        pltpu.make_async_copy(w.at[piece(at)], stored.at[piece(at)], sems.at[at])
        for at in range(parts)
    ]
    for at in range(ahead):
        copies[at].start()
    for at in range(4):
        start = pl.multiple_of(order[at] * share, share)
        turned[pl.ds(at * share, share)] = grad[pl.ds(start, share)]
    for at in range(parts):
        if at + ahead < parts:
            copies[at + ahead].start()
        copies[at].wait()
        made = dot_nt(turned[...], stored[piece(at)])
        held[:, piece(at)] = made[: 2 * share]
        sent[:, piece(at)] = made[2 * share :].astype(BF16)


def input_grad(order, grad, w_whole):
    rows, columns = grad.shape
    width = w_whole.shape[0]
    return pl.pallas_call(
        input_grad_kernel,
        in_specs=[SMEM, VMEM, pl.BlockSpec(memory_space=pl.ANY)],
        out_specs=[VMEM] * 2,
        out_shape=[
            jax.ShapeDtypeStruct((rows // 2, width), BF16),
            jax.ShapeDtypeStruct((rows // 2, width), F32),
        ],
        scratch_shapes=[
            pltpu.VMEM((rows, columns), BF16),
            pltpu.VMEM((width, columns), BF16),
            pltpu.SemaphoreType.DMA((6,)),
        ],
        compiler_params=pltpu.CompilerParams(vmem_limit_bytes=WIDE_LIMIT),
        cost_estimate=QUICK,
        name="input_grad",
    )(order, grad, w_whole)


def finish_kernel(held, first, second, tokens, mod_scale, out):
    floats = tokens[...].astype(F32)
    centred = floats - jnp.mean(floats, axis=-1, keepdims=True)
    inverse = lax.rsqrt(jnp.mean(centred * centred, axis=-1, keepdims=True) + EPS)
    unit = centred * inverse
    near = pl.ds(0, out.shape[0])
    total = held[near] + first[near].astype(F32) + second[...].astype(F32)
    scaled = total * (1.0 + mod_scale[...])
    inner = scaled - jnp.mean(scaled, axis=-1, keepdims=True)
    along = jnp.mean(scaled * unit, axis=-1, keepdims=True)
    out[...] = (inverse * (inner - unit * along)).astype(BF16)


def after(*values):
    return lax.optimization_barrier(values)


def added(*parts):
    total = parts[0].astype(F32)
    for part in parts[1:]:
        total = total + part.astype(F32)
    return total.astype(BF16)


def local(tokens, tile_anchor, partners, weight, mod_shift, mod_scale, q_gain, k_gain, grad_out):
    rows = tokens.shape[0]
    heads, dim = weight.shape[1], weight.shape[3]
    columns = heads * 3 * dim
    score_scale = 1.0 / math.sqrt(dim)
    tile_total = lax.axis_size("dp")
    here = lax.axis_index("dp")
    slab, t, h = here // 4, here // 2 % 2, here % 2
    far = jnp.where(slab % 2 == 0, slab - 1, slab + 1)
    listed = partners[0]

    def flags_of(*spots):
        ids = jnp.stack([4 * s + 2 * (t ^ dt) + (h ^ dc) for s, dt, dc in spots])
        inside = jnp.logical_and(ids >= 0, ids < tile_total)
        return jnp.logical_and(
            inside, jnp.any(listed[None, :] == ids[:, None], axis=1)
        ).astype(jnp.int32)

    (w_local,) = call(
        pack_kernel, "pack", [weight.transpose(1, 2, 0, 3)], [((weight.shape[0], columns), BF16)]
    )
    w_whole = lax.all_gather(w_local, "dp", axis=0, tiled=True)

    unit_rows = normalize(tokens)
    normed = (unit_rows * (1.0 + mod_scale) + mod_shift).astype(BF16)
    tables = rope_tables(tile_anchor[0], dim)
    head_at = lax.axis_index("head")
    chip_order = jnp.concatenate([reach(here // 2, ORDERS[n], h) for n in range(2)])
    head_order = reach(head_at, HEAD_ORDERS, h)
    tokens_share = lax.dynamic_slice_in_dim(tokens, head_at * (rows // 4), rows // 4, 0)
    by_owner = normed.T.reshape(16, 2, weight.shape[0], rows)
    mine = lax.dynamic_index_in_dim(by_owner, h, 1, keepdims=False)
    other = move(lax.dynamic_index_in_dim(by_owner, 1 - h, 1, keepdims=False), CORE)
    grad = grad_out.transpose(1, 0, 2)
    normed, mine, other, grad, tokens_share, *tables = after(
        normed, mine, other, grad, tokens_share, *tables
    )

    q, own, raw = project(
        normed, w_whole, tables, q_gain, k_gain, heads, dim, score_scale * LOG2E
    )

    pal = slab ^ 1
    f_own = flags_of((slab, 0, 0), (slab, 0, 1))
    f_side = flags_of((slab, 1, 0), (slab, 1, 1))
    f_near = flags_of((pal, 1, 0), (pal, 1, 1))
    f_near1 = flags_of((pal, 0, 0), (pal, 0, 1))
    f_edge = flags_of((far, 1, 0), (far, 1, 1))
    f_edge1 = flags_of((far, 0, 0), (far, 0, 1))
    join = lambda *f: jnp.concatenate(f)

    edge = move(own, HALO)
    side = move(own, Z1)
    own_c = move(own, CORE)
    (acc,) = attend(f_own, q, [own, own_c])
    edge, acc, own_then = after(edge, acc, own)
    near = move(own_then, Z3)
    edge1 = move(edge, Z1)
    edge_c = move(edge, CORE)
    side_c = move(side, CORE)
    (acc,) = attend(join(f_edge, f_side), q, [edge, edge_c, side, side_c], acc)
    near, acc = after(near, acc)
    near1 = move(jnp.where(h == 0, near, side), ACROSS)
    near_c = move(near, CORE)
    edge1_c = move(edge1, CORE)
    (acc,) = attend(join(f_near, f_edge1), q, [near, near_c, edge1, edge1_c], acc)
    near1, acc = after(near1, acc)
    near1_c = move(near1, CORE)
    attn_out, grad_ext = attend(f_near1, q, [near1, near1_c], acc, grad)

    dq, (d_near1_c,) = differentiate(f_near1[1:], q, grad_ext, [near1_c])
    near1_swap = move(d_near1_c, CORE)
    dq, (d_near1,) = differentiate(f_near1[:1], q, grad_ext, [near1], dq)
    near1_sum = added(d_near1, near1_swap)
    near1_back = move(near1_sum, ACROSS)
    near1_sum, dq = after(near1_sum, dq)
    dq, (d_near, d_near_c) = differentiate(f_near, q, grad_ext, [near, near_c], dq)
    near_swap = move(d_near_c, CORE)
    dq, (d_edge1, d_edge1_c) = differentiate(f_edge1, q, grad_ext, [edge1, edge1_c], dq)
    edge1_swap = move(d_edge1_c, CORE)
    near1_back, dq = after(near1_back, dq)
    dq, (d_edge, d_edge_c, d_side, d_side_c) = differentiate(
        join(f_edge, f_side), q, grad_ext, [edge, edge_c, side, side_c], dq, LONG
    )
    edge_swap = move(d_edge_c, CORE)
    side_swap = move(d_side_c, CORE)
    near_swap, edge1_swap, dq = after(near_swap, edge1_swap, dq)
    none = jnp.zeros((), BF16)
    near_sum = added(d_near, near_swap, jnp.where(h == 0, near1_back, none))
    near_back = move(near_sum, Z3)
    edge1_sum = added(d_edge1, edge1_swap)
    edge1_back = move(edge1_sum, Z1)
    near_sum, edge1_sum, dq = after(near_sum, edge1_sum, dq)
    dq, (d_own, d_own_c) = differentiate(f_own, q, grad_ext, [own, own_c], dq)
    near_back, edge1_back, edge_swap, side_swap, dq, d_own_c = after(
        near_back, edge1_back, edge_swap, side_swap, dq, d_own_c
    )
    edge_sum = added(d_edge, edge_swap, edge1_back)
    edge_back = move(edge_sum, HALO)
    side_sum = added(d_side, side_swap, jnp.where(h == 0, none, near1_back))
    side_back = move(side_sum, Z1)
    own_back = move(d_own_c, CORE)

    grad_proj = pullback(
        raw,
        dq,
        tables,
        q_gain,
        k_gain,
        [d_own, own_back, side_back, near_back, edge_back],
        score_scale,
    )
    grad_proj_other = move(grad_proj, CORE)
    width = weight.shape[0]
    rows_sent, rows_held = input_grad(head_order, grad_proj, w_whole)
    rows_first = head_exchange(rows_sent, 0)
    grad_proj_other, rows_held = after(grad_proj_other, rows_held)

    lhs = [chip_order, mine, other, grad_proj, grad_proj_other]
    shapes = lambda chips, kind: [((chips * width // 2, columns), kind)] * 2
    sent = call(functools.partial(weigh_kernel, 8), "weigh_far", lhs, shapes(8, BF16), smem=1)
    came = [exchange(sent[stream], stream, 0) for stream in range(2)]
    held = call(functools.partial(weigh_kernel, 0), "weigh_near", lhs, shapes(8, F32), smem=1)
    for step in (1, 2, 3):
        *sent, held_a, held_b = call(
            halve_kernel,
            "halve",
            [*held, *came],
            shapes(8 >> step, BF16) + shapes(8 >> step, F32),
        )
        held = [held_a, held_b]
        came = [exchange(sent[stream], stream, step) for stream in range(2)]
        if step == 1:
            rows_first, *held = after(rows_first, *held)
            (rows_next,) = call(
                merge_kernel, "merge_rows", [rows_held, rows_first], [((rows // 4, tokens.shape[1]), BF16)]
            )
            rows_second = head_exchange(rows_next, 1)
            rows_next, *held = after(rows_next, *held)
    (grad_tokens,) = call(
        finish_kernel,
        "finish",
        [rows_held, rows_first, rows_second, tokens_share, mod_scale[None, :]],
        [(tokens_share.shape, BF16)],
    )
    grad_tokens, *held = after(grad_tokens, *held)
    (grad_weight,) = call(
        settle_kernel, "settle", [*held, *came], [((heads, 3, width, dim), F32)]
    )
    return (
        attn_out.transpose(1, 0, 2),
        grad_tokens,
        grad_weight.transpose(2, 0, 1, 3),
    )


def solution(mesh):
    return jax.shard_map(
        local,
        mesh=mesh,
        in_specs=(
            P("dp", None),
            P("dp", None),
            P("dp", None),
            P("dp", "head", None, None),
            P(),
            P(),
            P(),
            P(),
            P("dp", "head", None),
        ),
        out_specs=(P("dp", "head", None), P(("dp", "head"), None), P("dp", "head", None, None)),
        check_vma=False,
    )
```

```python
import functools
import math

import jax
import jax.numpy as jnp
from jax import lax
from jax.experimental import pallas as pl
from jax.experimental.pallas import tpu as pltpu
from jax.sharding import PartitionSpec as P

TT = 6
TH = 8
TW = 8
THETA = 256.0
EPS = 1e-06
F32 = jnp.float32
LONG = pl.CostEstimate(flops=20_000_000_000, bytes_accessed=30_000_000, transcendentals=0)
QUICK = pl.CostEstimate(flops=1000, bytes_accessed=1000, transcendentals=0)
BF16 = jnp.bfloat16
LOG2E = 1.4426950408889634
LN2 = 0.6931471805599453
VMEM_LIMIT = 32 * 1024 * 1024
PROJECT_LIMIT = 58 * 1024 * 1024
WIDE_LIMIT = 58 * 1024 * 1024

CHIPS = [(x, z, c) for x in range(4) for z in range(4) for c in range(2)]


def place(x, z, c):
    return (x * 4 + z) * 2 + c


def pairs_of(move):
    return [(place(*p), place(*move(*p))) for p in CHIPS]


CORE = pairs_of(lambda x, z, c: (x, z, 1 - c))
Z1 = pairs_of(lambda x, z, c: (x, z ^ 1, c))
Z3 = pairs_of(lambda x, z, c: (x, z ^ 3, c))
HALO = [
    (place(x, z, c), place(x - 1 if z < 2 else x + 1, z ^ 3, c))
    for x, z, c in CHIPS
    if 0 <= (x - 1 if z < 2 else x + 1) < 4
]
Z_RING = [pairs_of(lambda x, z, c, k=k: (x, (z + k) % 4, c)) for k in range(4)]
ORDERS = (((4, 1, 12, 3), (12, 3, 4, 1)), ((1, 12, 3, 4), (3, 4, 1, 12)))
HEAD_ORDERS = ((1, 3), (3, 1))


def exchange(value, stream, step):
    return lax.ppermute(
        value,
        "dp",
        [
            (chip * 2 + c, (chip ^ ORDERS[stream][c][step]) * 2 + c)
            for chip in range(16)
            for c in range(2)
        ],
    )


def head_exchange(value, step):
    return lax.ppermute(
        value,
        ("dp", "head"),
        [
            (device * 4 + y, device * 4 + (y ^ HEAD_ORDERS[device % 2][step]))
            for device in range(32)
            for y in range(4)
        ],
    )


def reach(start, masks, core):
    steps = len(masks[0])
    table = []
    for c in range(2):
        row = []
        for at in range(2**steps):
            mask = 0
            for step in range(steps):
                if at >> (steps - 1 - step) & 1:
                    mask ^= masks[c][step]
            row.append(mask)
        table.append(row)
    return start ^ jnp.where(core == 0, jnp.array(table[0]), jnp.array(table[1])).astype(jnp.int32)


ACROSS = pairs_of(lambda x, z, c: (x, z ^ (3 if c else 1), c))


def move(value, pairs):
    return lax.ppermute(value, "dp", pairs)


def rope_tables(anchor, head_dim):
    token_ids = jnp.arange(TT * TH * TW, dtype=jnp.int32)[:, None]
    frames = anchor[0] + token_ids // (TH * TW)
    image_rows = anchor[1] + token_ids // TW % TH
    image_cols = anchor[2] + token_ids % TW
    section_t = head_dim // 8
    section_s = (head_dim - section_t) // 2
    channel = jnp.arange(head_dim, dtype=jnp.int32)[None, :]
    first = channel < section_t
    second = channel < section_t + section_s
    section_start = jnp.where(first, 0, jnp.where(second, section_t, section_t + section_s))
    section_len = jnp.where(first, section_t, section_s)
    pair_index = ((channel - section_start) // 2).astype(F32)
    frequency = THETA ** (-2.0 * pair_index / section_len.astype(F32))
    position = jnp.where(first, frames, jnp.where(second, image_rows, image_cols)).astype(F32)
    angles = position * frequency
    sine = jnp.sin(angles)
    even = channel % 2 == 0
    return (jnp.cos(angles), jnp.where(even, -sine, 0.0), jnp.where(even, 0.0, sine))


def normalize(tokens):
    floats = tokens.astype(F32)
    centred = floats - jnp.mean(floats, axis=-1, keepdims=True)
    inverse = lax.rsqrt(jnp.mean(centred * centred, axis=-1, keepdims=True) + EPS)
    return centred * inverse


def dot_nt(a, b):
    return lax.dot_general(a, b, (((1,), (1,)), ((), ())), preferred_element_type=F32)


def dot_tn(a, b):
    return lax.dot_general(a, b, (((0,), (0,)), ((), ())), preferred_element_type=F32)


def dot_nn(a, b):
    return jnp.dot(a, b, preferred_element_type=F32)


def turn(values, cosine, sine_up, sine_dn, sign):
    up = pltpu.roll(values, 127, 1)
    dn = pltpu.roll(values, 1, 1)
    return values * cosine + sign * (up * sine_up + dn * sine_dn)


def project_kernel(scale, place_of, normed, cos, sup, sdn, qg, kg, *refs):
    pieces = refs[:8]
    q_out, kv_out, raw_out, w_out, held, sems, out_sem = refs[8:]
    count, height = pieces[0].shape[:2]
    copies = []
    for group, piece in enumerate(pieces):
        for at in range(count):
            index = group * count + at
            row = pl.multiple_of(place_of[index], 16)
            copies.append(
                pltpu.make_async_copy(piece.at[at], held.at[pl.ds(row, height)], sems.at[index])
            )
    for copy in copies:
        copy.start()
    c, su, sd = cos[...], sup[...], sdn[...]
    for copy in copies:
        copy.wait()
    keep = pltpu.make_async_copy(held, w_out, out_sem)
    keep.start()
    for h in range(q_out.shape[0]):
        made = dot_nn(normed[...], held[:, 384 * h : 384 * (h + 1)])
        s0, s1, s2 = (made[:, 128 * n : 128 * (n + 1)] for n in range(3))
        query = s0 * lax.rsqrt(jnp.mean(s0 * s0, axis=-1, keepdims=True) + EPS) * qg[...]
        key = s1 * lax.rsqrt(jnp.mean(s1 * s1, axis=-1, keepdims=True) + EPS) * kg[...]
        q_out[h] = (turn(query, c, su, sd, 1.0) * scale).astype(BF16)
        kv_out[0, h] = turn(key, c, su, sd, 1.0).astype(BF16)
        kv_out[1, h] = s2.astype(BF16)
        raw_out[0, h] = s0
        raw_out[1, h] = s1
    keep.wait()


def project(place_of, normed, pieces, tables, q_gain, k_gain, heads, dim, scale):
    rows, width = normed.shape
    anywhere = pl.BlockSpec(memory_space=pl.ANY)
    return pl.pallas_call(
        functools.partial(project_kernel, scale),
        in_specs=[SMEM] + [VMEM] * 6 + [anywhere] * len(pieces),
        out_specs=[VMEM] * 3 + [anywhere],
        out_shape=[
            jax.ShapeDtypeStruct((heads, rows, dim), BF16),
            jax.ShapeDtypeStruct((2, heads, rows, dim), BF16),
            jax.ShapeDtypeStruct((2, heads, rows, dim), F32),
            jax.ShapeDtypeStruct((width, heads * 3 * dim), BF16),
        ],
        scratch_shapes=[
            pltpu.VMEM((width, heads * 3 * dim), BF16),
            pltpu.SemaphoreType.DMA((len(pieces) * pieces[0].shape[0],)),
            pltpu.SemaphoreType.DMA,
        ],
        compiler_params=pltpu.CompilerParams(vmem_limit_bytes=PROJECT_LIMIT),
        cost_estimate=QUICK,
        name="project",
    )(place_of, normed, *tables, q_gain[None, :], k_gain[None, :], *pieces)


VMEM = pl.BlockSpec(memory_space=pltpu.VMEM)
SMEM = pl.BlockSpec(memory_space=pltpu.SMEM)


def forward_kernel(count, first, last, *refs):
    flags, q = refs[:2]
    tiles = refs[2 : 2 + count]
    rest = refs[2 + count :]
    heads, rows, dim = q.shape
    if first:
        acc = rest[0] if not last else None
    if first:
        acc[...] = jnp.zeros(acc.shape, F32)
    elif not last:
        before, acc = rest
        acc[...] = before[...]
    else:
        before, grad, attn_out, grad_ext, acc = rest
        acc[...] = before[...]
    ones = jnp.ones((rows, dim), BF16)
    for at, kv in enumerate(tiles):

        @pl.when(flags[at] != 0)
        def attend(kv=kv):
            for h in range(heads):
                weights = jnp.exp2(dot_nt(q[h], kv[0, h])).astype(BF16)
                acc[h] += dot_nn(weights, jnp.concatenate([kv[1, h], ones], axis=1))

    if last:
        lane = lax.broadcasted_iota(jnp.int32, (rows, dim), 1)
        for h in range(heads):
            share = 1.0 / acc[h, :, dim : dim + 1]
            attn = (acc[h, :, :dim] * share).astype(BF16)
            attn_out[h] = attn
            g = grad[h].astype(F32)
            delta = jnp.sum(g * attn.astype(F32), axis=-1, keepdims=True) * share
            high = delta.astype(BF16).astype(F32)
            low = delta - high
            grad_ext[h, :, :dim] = (g * share).astype(BF16)
            grad_ext[h, :, dim:] = jnp.where(
                lane == 0, high, jnp.where(lane == 1, low, 0.0)
            ).astype(BF16)


def attend(flags, q, tiles, before=None, grad=None):
    heads, rows, dim = q.shape
    count = len(tiles)
    acc_shape = jax.ShapeDtypeStruct((heads, rows, 2 * dim), F32)
    last = grad is not None
    operands = [flags, q, *tiles]
    scratch = []
    if before is not None:
        operands.append(before)
    out_shape = [acc_shape]
    if last:
        operands.append(grad)
        out_shape = [
            jax.ShapeDtypeStruct((heads, rows, dim), BF16),
            jax.ShapeDtypeStruct((heads, rows, 2 * dim), BF16),
        ]
        scratch = [pltpu.VMEM(acc_shape.shape, F32)]
    return pl.pallas_call(
        functools.partial(forward_kernel, count, before is None, last),
        in_specs=[SMEM] + [VMEM] * (len(operands) - 1),
        out_specs=[VMEM] * len(out_shape),
        out_shape=out_shape,
        scratch_shapes=scratch,
        compiler_params=pltpu.CompilerParams(vmem_limit_bytes=VMEM_LIMIT),
        cost_estimate=QUICK,
        name="attend",
    )(*operands)


def backward_kernel(count, first, *refs):
    flags, q, grad_ext = refs[:3]
    tiles = refs[3 : 3 + count]
    rest = refs[3 + count :]
    heads, rows, dim = q.shape
    if first:
        dq, outs = rest[0], rest[1:]
        dq[...] = jnp.zeros(dq.shape, F32)
    else:
        before, dq, outs = rest[0], rest[1], rest[2:]
        dq[...] = before[...]
    lane = lax.broadcasted_iota(jnp.int32, (rows, dim), 1)
    minus = jnp.where(lane < 2, -1.0, 0.0).astype(BF16)
    for at, (kv, out) in enumerate(zip(tiles, outs)):

        @pl.when(flags[at] != 0)
        def differentiate(kv=kv, out=out):
            for h in range(heads):
                key = kv[0, h]
                exps = jnp.exp2(dot_nt(key, q[h]))
                inner = dot_nt(jnp.concatenate([kv[1, h], minus], axis=1), grad_ext[h])
                dscore = (exps * inner).astype(BF16)
                out[1, h] = dot_nn(exps.astype(BF16), grad_ext[h, :, :dim]).astype(BF16)
                out[0, h] = (dot_nn(dscore, q[h]) * LN2).astype(BF16)
                dq[h] += dot_tn(dscore, key)

        @pl.when(flags[at] == 0)
        def unused(out=out):
            out[...] = jnp.zeros(out.shape, BF16)


def differentiate(flags, q, grad_ext, tiles, before=None, cost=QUICK):
    heads, rows, dim = q.shape
    count = len(tiles)
    operands = [flags, q, grad_ext, *tiles]
    if before is not None:
        operands.append(before)
    result = pl.pallas_call(
        functools.partial(backward_kernel, count, before is None),
        in_specs=[SMEM] + [VMEM] * (len(operands) - 1),
        out_specs=[VMEM] * (1 + count),
        out_shape=[jax.ShapeDtypeStruct((heads, rows, dim), F32)]
        + [jax.ShapeDtypeStruct((2, heads, rows, dim), BF16)] * count,
        compiler_params=pltpu.CompilerParams(vmem_limit_bytes=VMEM_LIMIT),
        cost_estimate=cost,
        name="differentiate",
    )(*operands)
    return result[0], result[1:]


def pullback_kernel(scale, raw, dq, cos, sup, sdn, qg, kg, *refs):
    parts, out = refs[:-1], refs[-1]
    heads, rows, dim = dq.shape
    c, su, sd = cos[...], sup[...], sdn[...]

    def through_norm(grad, s, gain):
        grad = turn(grad, c, su, sd, -1.0) * gain
        inverse = lax.rsqrt(jnp.mean(s * s, axis=-1, keepdims=True) + EPS)
        along = jnp.mean(grad * s, axis=-1, keepdims=True) * (inverse * inverse)
        return inverse * (grad - s * along)

    for h in range(heads):
        key = parts[0][0, h].astype(F32)
        value = parts[0][1, h].astype(F32)
        for part in parts[1:]:
            key += part[0, h].astype(F32)
            value += part[1, h].astype(F32)
        base = 3 * dim * h
        out[:, base : base + dim] = through_norm(dq[h] * scale, raw[0, h], qg[...]).astype(BF16)
        out[:, base + dim : base + 2 * dim] = through_norm(key, raw[1, h], kg[...]).astype(BF16)
        out[:, base + 2 * dim : base + 3 * dim] = value.astype(BF16)


def pullback(raw, dq, tables, q_gain, k_gain, parts, scale):
    heads, rows, dim = dq.shape
    return pl.pallas_call(
        functools.partial(pullback_kernel, scale),
        in_specs=[VMEM] * (7 + len(parts)),
        out_specs=VMEM,
        out_shape=jax.ShapeDtypeStruct((rows, heads * 3 * dim), BF16),
        compiler_params=pltpu.CompilerParams(vmem_limit_bytes=VMEM_LIMIT),
        cost_estimate=QUICK,
        name="pullback",
    )(raw, dq, *tables, q_gain[None, :], k_gain[None, :], *parts)


def call(kernel, name, operands, shapes, smem=0, scratch=(), flops=1_000_000):
    return pl.pallas_call(
        kernel,
        in_specs=[SMEM] * smem + [VMEM] * (len(operands) - smem),
        out_specs=[VMEM] * len(shapes),
        out_shape=[jax.ShapeDtypeStruct(shape, kind) for shape, kind in shapes],
        scratch_shapes=list(scratch),
        compiler_params=pltpu.CompilerParams(vmem_limit_bytes=VMEM_LIMIT),
        cost_estimate=QUICK,
        name=name,
    )(*operands)


def weigh_kernel(first, order, mine, other, grad, grad_other, *outs):
    half = mine.shape[1] // 2
    for stream, out in enumerate(outs):
        rows = pl.ds(stream * half, half)
        chips = [order[16 * stream + first + at] for at in range(8)]
        left = jnp.concatenate([mine[chip, rows] for chip in chips], axis=0)
        right = jnp.concatenate([other[chip, rows] for chip in chips], axis=0)
        made = dot_nn(left, grad[...]) + dot_nn(right, grad_other[...])
        out[...] = made.astype(out.dtype)


def halve_kernel(*refs):
    for stream in range(2):
        held, came, sent, kept = (refs[2 * n + stream] for n in range(4))
        half = sent.shape[0]
        low, high = pl.ds(0, half), pl.ds(half, half)
        sent[...] = (held[high] + came[high].astype(F32)).astype(BF16)
        kept[...] = held[low] + came[low].astype(F32)


def settle_kernel(held_a, held_b, came_a, came_b, out):
    for stream, (held, came) in enumerate(((held_a, came_a), (held_b, came_b))):
        total = held[...] + came[...].astype(F32)
        half = total.shape[0]
        for at in range(9):
            out[at // 3, at % 3, pl.ds(stream * half, half)] = total[:, at * 128 : (at + 1) * 128]


def merge_kernel(held, came, out):
    share = out.shape[0]
    out[...] = (held[pl.ds(share, share)] + came[pl.ds(share, share)].astype(F32)).astype(BF16)


def pack_kernel(weight, out):
    for at in range(9):
        out[:, at * 128 : (at + 1) * 128] = weight[at // 3, at % 3].astype(BF16)


def input_grad_kernel(order, grad, w, sent, held, turned, stored, sems):
    share = grad.shape[0] // 4
    parts = sems.shape[0]
    chunk = w.shape[0] // parts
    ahead = 2

    def piece(at):
        return slice(at * chunk, (at + 1) * chunk)

    copies = [
        pltpu.make_async_copy(w.at[piece(at)], stored.at[piece(at)], sems.at[at])
        for at in range(parts)
    ]
    for at in range(ahead):
        copies[at].start()
    for at in range(4):
        start = pl.multiple_of(order[at] * share, share)
        turned[pl.ds(at * share, share)] = grad[pl.ds(start, share)]
    for at in range(parts):
        if at + ahead < parts:
            copies[at + ahead].start()
        copies[at].wait()
        made = dot_nt(turned[...], stored[piece(at)])
        held[:, piece(at)] = made[: 2 * share]
        sent[:, piece(at)] = made[2 * share :].astype(BF16)


def input_grad(order, grad, w_whole):
    rows, columns = grad.shape
    width = w_whole.shape[0]
    return pl.pallas_call(
        input_grad_kernel,
        in_specs=[SMEM, VMEM, pl.BlockSpec(memory_space=pl.ANY)],
        out_specs=[VMEM] * 2,
        out_shape=[
            jax.ShapeDtypeStruct((rows // 2, width), BF16),
            jax.ShapeDtypeStruct((rows // 2, width), F32),
        ],
        scratch_shapes=[
            pltpu.VMEM((rows, columns), BF16),
            pltpu.VMEM((width, columns), BF16),
            pltpu.SemaphoreType.DMA((6,)),
        ],
        compiler_params=pltpu.CompilerParams(vmem_limit_bytes=WIDE_LIMIT),
        cost_estimate=QUICK,
        name="input_grad",
    )(order, grad, w_whole)


def finish_kernel(held, first, second, tokens, mod_scale, out):
    floats = tokens[...].astype(F32)
    centred = floats - jnp.mean(floats, axis=-1, keepdims=True)
    inverse = lax.rsqrt(jnp.mean(centred * centred, axis=-1, keepdims=True) + EPS)
    unit = centred * inverse
    near = pl.ds(0, out.shape[0])
    total = held[near] + first[near].astype(F32) + second[...].astype(F32)
    scaled = total * (1.0 + mod_scale[...])
    inner = scaled - jnp.mean(scaled, axis=-1, keepdims=True)
    along = jnp.mean(scaled * unit, axis=-1, keepdims=True)
    out[...] = (inverse * (inner - unit * along)).astype(BF16)


def after(*values):
    return lax.optimization_barrier(values)


def added(*parts):
    total = parts[0].astype(F32)
    for part in parts[1:]:
        total = total + part.astype(F32)
    return total.astype(BF16)


def local(tokens, tile_anchor, partners, weight, mod_shift, mod_scale, q_gain, k_gain, grad_out):
    rows = tokens.shape[0]
    heads, dim = weight.shape[1], weight.shape[3]
    columns = heads * 3 * dim
    score_scale = 1.0 / math.sqrt(dim)
    tile_total = lax.axis_size("dp")
    here = lax.axis_index("dp")
    slab, t, h = here // 4, here // 2 % 2, here % 2
    far = jnp.where(slab % 2 == 0, slab - 1, slab + 1)
    listed = partners[0]

    def flags_of(*spots):
        ids = jnp.stack([4 * s + 2 * (t ^ dt) + (h ^ dc) for s, dt, dc in spots])
        inside = jnp.logical_and(ids >= 0, ids < tile_total)
        return jnp.logical_and(
            inside, jnp.any(listed[None, :] == ids[:, None], axis=1)
        ).astype(jnp.int32)

    (w_local,) = call(
        pack_kernel, "pack", [weight.transpose(1, 2, 0, 3)], [((weight.shape[0], columns), BF16)]
    )
    share_height = weight.shape[0]
    half = share_height // 2
    near_pieces, far_pieces = [], []
    for stream in range(2):
        piece = w_local[stream * half : (stream + 1) * half][None]
        for step in (3, 2, 1):
            piece = jnp.concatenate([piece, exchange(piece, stream, step)], axis=0)
        near_pieces.append(piece)
    far_pieces = [exchange(piece, stream, 0) for stream, piece in enumerate(near_pieces)]
    pieces = []
    for stream in range(2):
        pieces += [near_pieces[stream], far_pieces[stream]]
    pieces += [move(piece, CORE) for piece in pieces]
    place_of = jnp.concatenate(
        [
            (reach(here // 2, ORDERS[stream], core) * 2 + core) * share_height + stream * half
            for core in (h, 1 - h)
            for stream in range(2)
        ]
    ).astype(jnp.int32)

    tokens, tile_anchor, *near_pieces = after(tokens, tile_anchor, *near_pieces)
    unit_rows = normalize(tokens)
    normed = (unit_rows * (1.0 + mod_scale) + mod_shift).astype(BF16)
    tables = rope_tables(tile_anchor[0], dim)
    head_at = lax.axis_index("head")
    chip_order = jnp.concatenate([reach(here // 2, ORDERS[n], h) for n in range(2)])
    head_order = reach(head_at, HEAD_ORDERS, h)
    tokens_share = lax.dynamic_slice_in_dim(tokens, head_at * (rows // 4), rows // 4, 0)
    by_owner = normed.T.reshape(16, 2, weight.shape[0], rows)
    mine = lax.dynamic_index_in_dim(by_owner, h, 1, keepdims=False)
    other = move(lax.dynamic_index_in_dim(by_owner, 1 - h, 1, keepdims=False), CORE)
    grad = grad_out.transpose(1, 0, 2)
    normed, mine, other, grad, tokens_share, *tables = after(
        normed, mine, other, grad, tokens_share, *tables
    )

    q, own, raw, w_whole = project(
        place_of, normed, pieces, tables, q_gain, k_gain, heads, dim, score_scale * LOG2E
    )

    pal = slab ^ 1
    f_own = flags_of((slab, 0, 0), (slab, 0, 1))
    f_side = flags_of((slab, 1, 0), (slab, 1, 1))
    f_near = flags_of((pal, 1, 0), (pal, 1, 1))
    f_near1 = flags_of((pal, 0, 0), (pal, 0, 1))
    f_edge = flags_of((far, 1, 0), (far, 1, 1))
    f_edge1 = flags_of((far, 0, 0), (far, 0, 1))
    join = lambda *f: jnp.concatenate(f)

    edge = move(own, HALO)
    side = move(own, Z1)
    own_c = move(own, CORE)
    (acc,) = attend(f_own, q, [own, own_c])
    edge, acc, own_then = after(edge, acc, own)
    near = move(own_then, Z3)
    edge1 = move(edge, Z1)
    edge_c = move(edge, CORE)
    side_c = move(side, CORE)
    (acc,) = attend(join(f_edge, f_side), q, [edge, edge_c, side, side_c], acc)
    near, acc = after(near, acc)
    near1 = move(jnp.where(h == 0, near, side), ACROSS)
    near_c = move(near, CORE)
    edge1_c = move(edge1, CORE)
    (acc,) = attend(join(f_near, f_edge1), q, [near, near_c, edge1, edge1_c], acc)
    near1, acc = after(near1, acc)
    near1_c = move(near1, CORE)
    attn_out, grad_ext = attend(f_near1, q, [near1, near1_c], acc, grad)

    dq, (d_near1_c,) = differentiate(f_near1[1:], q, grad_ext, [near1_c])
    near1_swap = move(d_near1_c, CORE)
    dq, (d_near1,) = differentiate(f_near1[:1], q, grad_ext, [near1], dq)
    near1_sum = added(d_near1, near1_swap)
    near1_back = move(near1_sum, ACROSS)
    near1_sum, dq = after(near1_sum, dq)
    dq, (d_near, d_near_c) = differentiate(f_near, q, grad_ext, [near, near_c], dq)
    near_swap = move(d_near_c, CORE)
    dq, (d_edge1, d_edge1_c) = differentiate(f_edge1, q, grad_ext, [edge1, edge1_c], dq)
    edge1_swap = move(d_edge1_c, CORE)
    near1_back, dq = after(near1_back, dq)
    dq, (d_edge, d_edge_c, d_side, d_side_c) = differentiate(
        join(f_edge, f_side), q, grad_ext, [edge, edge_c, side, side_c], dq, LONG
    )
    edge_swap = move(d_edge_c, CORE)
    side_swap = move(d_side_c, CORE)
    near_swap, edge1_swap, dq = after(near_swap, edge1_swap, dq)
    none = jnp.zeros((), BF16)
    near_sum = added(d_near, near_swap, jnp.where(h == 0, near1_back, none))
    near_back = move(near_sum, Z3)
    edge1_sum = added(d_edge1, edge1_swap)
    edge1_back = move(edge1_sum, Z1)
    near_sum, edge1_sum, dq = after(near_sum, edge1_sum, dq)
    dq, (d_own, d_own_c) = differentiate(f_own, q, grad_ext, [own, own_c], dq)
    near_back, edge1_back, edge_swap, side_swap, dq, d_own_c = after(
        near_back, edge1_back, edge_swap, side_swap, dq, d_own_c
    )
    edge_sum = added(d_edge, edge_swap, edge1_back)
    edge_back = move(edge_sum, HALO)
    side_sum = added(d_side, side_swap, jnp.where(h == 0, none, near1_back))
    side_back = move(side_sum, Z1)
    own_back = move(d_own_c, CORE)

    grad_proj = pullback(
        raw,
        dq,
        tables,
        q_gain,
        k_gain,
        [d_own, own_back, side_back, near_back, edge_back],
        score_scale,
    )
    grad_proj_other = move(grad_proj, CORE)
    width = weight.shape[0]
    rows_sent, rows_held = input_grad(head_order, grad_proj, w_whole)
    rows_first = head_exchange(rows_sent, 0)
    grad_proj_other, rows_held = after(grad_proj_other, rows_held)

    lhs = [chip_order, mine, other, grad_proj, grad_proj_other]
    shapes = lambda chips, kind: [((chips * width // 2, columns), kind)] * 2
    sent = call(functools.partial(weigh_kernel, 8), "weigh_far", lhs, shapes(8, BF16), smem=1)
    came = [exchange(sent[stream], stream, 0) for stream in range(2)]
    held = call(functools.partial(weigh_kernel, 0), "weigh_near", lhs, shapes(8, F32), smem=1)
    for step in (1, 2, 3):
        *sent, held_a, held_b = call(
            halve_kernel,
            "halve",
            [*held, *came],
            shapes(8 >> step, BF16) + shapes(8 >> step, F32),
        )
        held = [held_a, held_b]
        came = [exchange(sent[stream], stream, step) for stream in range(2)]
        if step == 1:
            rows_first, *held = after(rows_first, *held)
            (rows_next,) = call(
                merge_kernel, "merge_rows", [rows_held, rows_first], [((rows // 4, tokens.shape[1]), BF16)]
            )
            rows_second = head_exchange(rows_next, 1)
            rows_next, *held = after(rows_next, *held)
    (grad_tokens,) = call(
        finish_kernel,
        "finish",
        [rows_held, rows_first, rows_second, tokens_share, mod_scale[None, :]],
        [(tokens_share.shape, BF16)],
    )
    grad_tokens, *held = after(grad_tokens, *held)
    (grad_weight,) = call(
        settle_kernel, "settle", [*held, *came], [((heads, 3, width, dim), F32)]
    )
    return (
        attn_out.transpose(1, 0, 2),
        grad_tokens,
        grad_weight.transpose(2, 0, 1, 3),
    )


def solution(mesh):
    return jax.shard_map(
        local,
        mesh=mesh,
        in_specs=(
            P("dp", None),
            P("dp", None),
            P("dp", None),
            P("dp", "head", None, None),
            P(),
            P(),
            P(),
            P(),
            P("dp", "head", None),
        ),
        out_specs=(P("dp", "head", None), P(("dp", "head"), None), P("dp", "head", None, None)),
        check_vma=False,
    )
```

```python
import functools
import math

import jax
import jax.numpy as jnp
from jax import lax
from jax.experimental import pallas as pl
from jax.experimental.pallas import tpu as pltpu
from jax.sharding import PartitionSpec as P

TT = 6
TH = 8
TW = 8
THETA = 256.0
EPS = 1e-06
F32 = jnp.float32
LONG = pl.CostEstimate(flops=20_000_000_000, bytes_accessed=30_000_000, transcendentals=0)
QUICK = pl.CostEstimate(flops=1000, bytes_accessed=1000, transcendentals=0)
BF16 = jnp.bfloat16
LOG2E = 1.4426950408889634
LN2 = 0.6931471805599453
VMEM_LIMIT = 32 * 1024 * 1024
PROJECT_LIMIT = 58 * 1024 * 1024
WIDE_LIMIT = 58 * 1024 * 1024

CHIPS = [(x, z, c) for x in range(4) for z in range(4) for c in range(2)]


def place(x, z, c):
    return (x * 4 + z) * 2 + c


def pairs_of(move):
    return [(place(*p), place(*move(*p))) for p in CHIPS]


CORE = pairs_of(lambda x, z, c: (x, z, 1 - c))
Z1 = pairs_of(lambda x, z, c: (x, z ^ 1, c))
Z3 = pairs_of(lambda x, z, c: (x, z ^ 3, c))
HALO = [
    (place(x, z, c), place(x - 1 if z < 2 else x + 1, z ^ 3, c))
    for x, z, c in CHIPS
    if 0 <= (x - 1 if z < 2 else x + 1) < 4
]
Z_RING = [pairs_of(lambda x, z, c, k=k: (x, (z + k) % 4, c)) for k in range(4)]
ORDERS = (((4, 1, 12, 3), (12, 3, 4, 1)), ((1, 12, 3, 4), (3, 4, 1, 12)))
HEAD_ORDERS = ((1, 3), (3, 1))


def exchange(value, stream, step):
    return lax.ppermute(
        value,
        "dp",
        [
            (chip * 2 + c, (chip ^ ORDERS[stream][c][step]) * 2 + c)
            for chip in range(16)
            for c in range(2)
        ],
    )


def head_exchange(value, step):
    return lax.ppermute(
        value,
        ("dp", "head"),
        [
            (device * 4 + y, device * 4 + (y ^ HEAD_ORDERS[device % 2][step]))
            for device in range(32)
            for y in range(4)
        ],
    )


def reach(start, masks, core):
    steps = len(masks[0])
    table = []
    for c in range(2):
        row = []
        for at in range(2**steps):
            mask = 0
            for step in range(steps):
                if at >> (steps - 1 - step) & 1:
                    mask ^= masks[c][step]
            row.append(mask)
        table.append(row)
    return start ^ jnp.where(core == 0, jnp.array(table[0]), jnp.array(table[1])).astype(jnp.int32)


ACROSS = pairs_of(lambda x, z, c: (x, z ^ (3 if c else 1), c))


def move(value, pairs):
    return lax.ppermute(value, "dp", pairs)


def rope_tables(anchor, head_dim):
    token_ids = jnp.arange(TT * TH * TW, dtype=jnp.int32)[:, None]
    frames = anchor[0] + token_ids // (TH * TW)
    image_rows = anchor[1] + token_ids // TW % TH
    image_cols = anchor[2] + token_ids % TW
    section_t = head_dim // 8
    section_s = (head_dim - section_t) // 2
    channel = jnp.arange(head_dim, dtype=jnp.int32)[None, :]
    first = channel < section_t
    second = channel < section_t + section_s
    section_start = jnp.where(first, 0, jnp.where(second, section_t, section_t + section_s))
    section_len = jnp.where(first, section_t, section_s)
    pair_index = ((channel - section_start) // 2).astype(F32)
    frequency = THETA ** (-2.0 * pair_index / section_len.astype(F32))
    position = jnp.where(first, frames, jnp.where(second, image_rows, image_cols)).astype(F32)
    angles = position * frequency
    sine = jnp.sin(angles)
    even = channel % 2 == 0
    return (jnp.cos(angles), jnp.where(even, -sine, 0.0), jnp.where(even, 0.0, sine))


def normalize(tokens):
    floats = tokens.astype(F32)
    centred = floats - jnp.mean(floats, axis=-1, keepdims=True)
    inverse = lax.rsqrt(jnp.mean(centred * centred, axis=-1, keepdims=True) + EPS)
    return centred * inverse


def dot_nt(a, b):
    return lax.dot_general(a, b, (((1,), (1,)), ((), ())), preferred_element_type=F32)


def dot_tn(a, b):
    return lax.dot_general(a, b, (((0,), (0,)), ((), ())), preferred_element_type=F32)


def dot_nn(a, b):
    return jnp.dot(a, b, preferred_element_type=F32)


def turn(values, cosine, sine_up, sine_dn, sign):
    up = pltpu.roll(values, 127, 1)
    dn = pltpu.roll(values, 1, 1)
    return values * cosine + sign * (up * sine_up + dn * sine_dn)


def project_kernel(scale, place_of, normed, cos, sup, sdn, qg, kg, *refs):
    pieces = refs[:8]
    q_out, kv_out, raw_out, w_out, held, sems, out_sem = refs[8:]
    count, height = pieces[0].shape[:2]
    copies = []
    for group, piece in enumerate(pieces):
        for at in range(count):
            index = group * count + at
            row = pl.multiple_of(place_of[index], 16)
            copies.append(
                pltpu.make_async_copy(piece.at[at], held.at[pl.ds(row, height)], sems.at[index])
            )
    for copy in copies:
        copy.start()
    c, su, sd = cos[...], sup[...], sdn[...]
    for copy in copies:
        copy.wait()
    keep = pltpu.make_async_copy(held, w_out, out_sem)
    keep.start()
    for h in range(q_out.shape[0]):
        made = dot_nn(normed[...], held[:, 384 * h : 384 * (h + 1)])
        s0, s1, s2 = (made[:, 128 * n : 128 * (n + 1)] for n in range(3))
        query = s0 * lax.rsqrt(jnp.mean(s0 * s0, axis=-1, keepdims=True) + EPS) * qg[...]
        key = s1 * lax.rsqrt(jnp.mean(s1 * s1, axis=-1, keepdims=True) + EPS) * kg[...]
        q_out[h] = (turn(query, c, su, sd, 1.0) * scale).astype(BF16)
        kv_out[0, h] = turn(key, c, su, sd, 1.0).astype(BF16)
        kv_out[1, h] = s2.astype(BF16)
        raw_out[0, h] = s0
        raw_out[1, h] = s1
    keep.wait()


def project(place_of, normed, pieces, tables, q_gain, k_gain, heads, dim, scale):
    rows, width = normed.shape
    anywhere = pl.BlockSpec(memory_space=pl.ANY)
    return pl.pallas_call(
        functools.partial(project_kernel, scale),
        in_specs=[SMEM] + [VMEM] * 6 + [anywhere] * len(pieces),
        out_specs=[VMEM] * 3 + [anywhere],
        out_shape=[
            jax.ShapeDtypeStruct((heads, rows, dim), BF16),
            jax.ShapeDtypeStruct((2, heads, rows, dim), BF16),
            jax.ShapeDtypeStruct((2, heads, rows, dim), F32),
            jax.ShapeDtypeStruct((width, heads * 3 * dim), BF16),
        ],
        scratch_shapes=[
            pltpu.VMEM((width, heads * 3 * dim), BF16),
            pltpu.SemaphoreType.DMA((len(pieces) * pieces[0].shape[0],)),
            pltpu.SemaphoreType.DMA,
        ],
        compiler_params=pltpu.CompilerParams(vmem_limit_bytes=PROJECT_LIMIT),
        cost_estimate=QUICK,
        name="project",
    )(place_of, normed, *tables, q_gain[None, :], k_gain[None, :], *pieces)


VMEM = pl.BlockSpec(memory_space=pltpu.VMEM)
SMEM = pl.BlockSpec(memory_space=pltpu.SMEM)


def forward_kernel(count, first, last, *refs):
    flags, q = refs[:2]
    tiles = refs[2 : 2 + count]
    rest = refs[2 + count :]
    heads, rows, dim = q.shape
    if first:
        acc = rest[0] if not last else None
    if first:
        acc[...] = jnp.zeros(acc.shape, F32)
    elif not last:
        before, acc = rest
        acc[...] = before[...]
    else:
        before, grad, attn_out, grad_ext, acc = rest
        acc[...] = before[...]
    ones = jnp.ones((rows, dim), BF16)
    for at, kv in enumerate(tiles):

        @pl.when(flags[at] != 0)
        def attend(kv=kv):
            for h in range(heads):
                weights = jnp.exp2(dot_nt(q[h], kv[0, h])).astype(BF16)
                acc[h] += dot_nn(weights, jnp.concatenate([kv[1, h], ones], axis=1))

    if last:
        lane = lax.broadcasted_iota(jnp.int32, (rows, dim), 1)
        for h in range(heads):
            share = 1.0 / acc[h, :, dim : dim + 1]
            attn = (acc[h, :, :dim] * share).astype(BF16)
            attn_out[h] = attn
            g = grad[h].astype(F32)
            delta = jnp.sum(g * attn.astype(F32), axis=-1, keepdims=True) * share
            high = delta.astype(BF16).astype(F32)
            low = delta - high
            grad_ext[h, :, :dim] = (g * share).astype(BF16)
            grad_ext[h, :, dim:] = jnp.where(
                lane == 0, high, jnp.where(lane == 1, low, 0.0)
            ).astype(BF16)


def attend(flags, q, tiles, before=None, grad=None):
    heads, rows, dim = q.shape
    count = len(tiles)
    acc_shape = jax.ShapeDtypeStruct((heads, rows, 2 * dim), F32)
    last = grad is not None
    operands = [flags, q, *tiles]
    scratch = []
    if before is not None:
        operands.append(before)
    out_shape = [acc_shape]
    if last:
        operands.append(grad)
        out_shape = [
            jax.ShapeDtypeStruct((heads, rows, dim), BF16),
            jax.ShapeDtypeStruct((heads, rows, 2 * dim), BF16),
        ]
        scratch = [pltpu.VMEM(acc_shape.shape, F32)]
    return pl.pallas_call(
        functools.partial(forward_kernel, count, before is None, last),
        in_specs=[SMEM] + [VMEM] * (len(operands) - 1),
        out_specs=[VMEM] * len(out_shape),
        out_shape=out_shape,
        scratch_shapes=scratch,
        compiler_params=pltpu.CompilerParams(vmem_limit_bytes=VMEM_LIMIT),
        cost_estimate=QUICK,
        name="attend",
    )(*operands)


def backward_kernel(count, first, *refs):
    flags, q, grad_ext = refs[:3]
    tiles = refs[3 : 3 + count]
    rest = refs[3 + count :]
    heads, rows, dim = q.shape
    if first:
        dq, outs = rest[0], rest[1:]
        dq[...] = jnp.zeros(dq.shape, F32)
    else:
        before, dq, outs = rest[0], rest[1], rest[2:]
        dq[...] = before[...]
    lane = lax.broadcasted_iota(jnp.int32, (rows, dim), 1)
    minus = jnp.where(lane < 2, -1.0, 0.0).astype(BF16)
    for at, (kv, out) in enumerate(zip(tiles, outs)):

        @pl.when(flags[at] != 0)
        def differentiate(kv=kv, out=out):
            for h in range(heads):
                key = kv[0, h]
                exps = jnp.exp2(dot_nt(key, q[h]))
                inner = dot_nt(jnp.concatenate([kv[1, h], minus], axis=1), grad_ext[h])
                dscore = (exps * inner).astype(BF16)
                out[1, h] = dot_nn(exps.astype(BF16), grad_ext[h, :, :dim]).astype(BF16)
                out[0, h] = (dot_nn(dscore, q[h]) * LN2).astype(BF16)
                dq[h] += dot_tn(dscore, key)

        @pl.when(flags[at] == 0)
        def unused(out=out):
            out[...] = jnp.zeros(out.shape, BF16)


def differentiate(flags, q, grad_ext, tiles, before=None, cost=QUICK):
    heads, rows, dim = q.shape
    count = len(tiles)
    operands = [flags, q, grad_ext, *tiles]
    if before is not None:
        operands.append(before)
    result = pl.pallas_call(
        functools.partial(backward_kernel, count, before is None),
        in_specs=[SMEM] + [VMEM] * (len(operands) - 1),
        out_specs=[VMEM] * (1 + count),
        out_shape=[jax.ShapeDtypeStruct((heads, rows, dim), F32)]
        + [jax.ShapeDtypeStruct((2, heads, rows, dim), BF16)] * count,
        compiler_params=pltpu.CompilerParams(vmem_limit_bytes=VMEM_LIMIT),
        cost_estimate=cost,
        name="differentiate",
    )(*operands)
    return result[0], result[1:]


def pullback_kernel(scale, raw, dq, cos, sup, sdn, qg, kg, *refs):
    parts, out = refs[:-1], refs[-1]
    heads, rows, dim = dq.shape
    c, su, sd = cos[...], sup[...], sdn[...]

    def through_norm(grad, s, gain):
        grad = turn(grad, c, su, sd, -1.0) * gain
        inverse = lax.rsqrt(jnp.mean(s * s, axis=-1, keepdims=True) + EPS)
        along = jnp.mean(grad * s, axis=-1, keepdims=True) * (inverse * inverse)
        return inverse * (grad - s * along)

    for h in range(heads):
        key = parts[0][0, h].astype(F32)
        value = parts[0][1, h].astype(F32)
        for part in parts[1:]:
            key += part[0, h].astype(F32)
            value += part[1, h].astype(F32)
        base = 3 * dim * h
        out[:, base : base + dim] = through_norm(dq[h] * scale, raw[0, h], qg[...]).astype(BF16)
        out[:, base + dim : base + 2 * dim] = through_norm(key, raw[1, h], kg[...]).astype(BF16)
        out[:, base + 2 * dim : base + 3 * dim] = value.astype(BF16)


def pullback(raw, dq, tables, q_gain, k_gain, parts, scale):
    heads, rows, dim = dq.shape
    return pl.pallas_call(
        functools.partial(pullback_kernel, scale),
        in_specs=[VMEM] * (7 + len(parts)),
        out_specs=VMEM,
        out_shape=jax.ShapeDtypeStruct((rows, heads * 3 * dim), BF16),
        compiler_params=pltpu.CompilerParams(vmem_limit_bytes=VMEM_LIMIT),
        cost_estimate=QUICK,
        name="pullback",
    )(raw, dq, *tables, q_gain[None, :], k_gain[None, :], *parts)


def call(kernel, name, operands, shapes, smem=0, scratch=(), flops=1_000_000):
    return pl.pallas_call(
        kernel,
        in_specs=[SMEM] * smem + [VMEM] * (len(operands) - smem),
        out_specs=[VMEM] * len(shapes),
        out_shape=[jax.ShapeDtypeStruct(shape, kind) for shape, kind in shapes],
        scratch_shapes=list(scratch),
        compiler_params=pltpu.CompilerParams(vmem_limit_bytes=VMEM_LIMIT),
        cost_estimate=QUICK,
        name=name,
    )(*operands)


def weigh_kernel(first, order, mine, other, grad, grad_other, *outs):
    half = mine.shape[1] // 2
    for stream, out in enumerate(outs):
        rows = pl.ds(stream * half, half)
        chips = [order[16 * stream + first + at] for at in range(8)]
        left = jnp.concatenate([mine[chip, rows] for chip in chips], axis=0)
        right = jnp.concatenate([other[chip, rows] for chip in chips], axis=0)
        made = dot_nn(left, grad[...]) + dot_nn(right, grad_other[...])
        out[...] = made.astype(out.dtype)


def halve_kernel(*refs):
    for stream in range(2):
        held, came, sent, kept = (refs[2 * n + stream] for n in range(4))
        half = sent.shape[0]
        low, high = pl.ds(0, half), pl.ds(half, half)
        sent[...] = (held[high] + came[high].astype(F32)).astype(BF16)
        kept[...] = held[low] + came[low].astype(F32)


def settle_kernel(held_a, held_b, came_a, came_b, out):
    for stream, (held, came) in enumerate(((held_a, came_a), (held_b, came_b))):
        total = held[...] + came[...].astype(F32)
        half = total.shape[0]
        for at in range(9):
            out[at // 3, at % 3, pl.ds(stream * half, half)] = total[:, at * 128 : (at + 1) * 128]


def merge_kernel(held, came, out):
    share = out.shape[0]
    out[...] = (held[pl.ds(share, share)] + came[pl.ds(share, share)].astype(F32)).astype(BF16)


def pack_kernel(weight, out):
    for at in range(9):
        out[:, at * 128 : (at + 1) * 128] = weight[at // 3, at % 3].astype(BF16)


def input_grad_kernel(order, grad, w, sent, held, turned, stored, sems):
    share = grad.shape[0] // 4
    parts = sems.shape[0]
    chunk = w.shape[0] // parts
    ahead = 2

    def piece(at):
        return slice(at * chunk, (at + 1) * chunk)

    copies = [
        pltpu.make_async_copy(w.at[piece(at)], stored.at[piece(at)], sems.at[at])
        for at in range(parts)
    ]
    for at in range(ahead):
        copies[at].start()
    for at in range(4):
        start = pl.multiple_of(order[at] * share, share)
        turned[pl.ds(at * share, share)] = grad[pl.ds(start, share)]
    for at in range(parts):
        if at + ahead < parts:
            copies[at + ahead].start()
        copies[at].wait()
        made = dot_nt(turned[...], stored[piece(at)])
        held[:, piece(at)] = made[: 2 * share]
        sent[:, piece(at)] = made[2 * share :].astype(BF16)


def input_grad(order, grad, w_whole):
    rows, columns = grad.shape
    width = w_whole.shape[0]
    return pl.pallas_call(
        input_grad_kernel,
        in_specs=[SMEM, VMEM, pl.BlockSpec(memory_space=pl.ANY)],
        out_specs=[VMEM] * 2,
        out_shape=[
            jax.ShapeDtypeStruct((rows // 2, width), BF16),
            jax.ShapeDtypeStruct((rows // 2, width), F32),
        ],
        scratch_shapes=[
            pltpu.VMEM((rows, columns), BF16),
            pltpu.VMEM((width, columns), BF16),
            pltpu.SemaphoreType.DMA((6,)),
        ],
        compiler_params=pltpu.CompilerParams(vmem_limit_bytes=WIDE_LIMIT),
        cost_estimate=QUICK,
        name="input_grad",
    )(order, grad, w_whole)


def finish_kernel(held, first, second, tokens, mod_scale, out):
    floats = tokens[...].astype(F32)
    centred = floats - jnp.mean(floats, axis=-1, keepdims=True)
    inverse = lax.rsqrt(jnp.mean(centred * centred, axis=-1, keepdims=True) + EPS)
    unit = centred * inverse
    near = pl.ds(0, out.shape[0])
    total = held[near] + first[near].astype(F32) + second[...].astype(F32)
    scaled = total * (1.0 + mod_scale[...])
    inner = scaled - jnp.mean(scaled, axis=-1, keepdims=True)
    along = jnp.mean(scaled * unit, axis=-1, keepdims=True)
    out[...] = (inverse * (inner - unit * along)).astype(BF16)


def after(*values):
    return lax.optimization_barrier(values)


def added(*parts):
    total = parts[0].astype(F32)
    for part in parts[1:]:
        total = total + part.astype(F32)
    return total.astype(BF16)


def local(tokens, tile_anchor, partners, weight, mod_shift, mod_scale, q_gain, k_gain, grad_out):
    rows = tokens.shape[0]
    heads, dim = weight.shape[1], weight.shape[3]
    columns = heads * 3 * dim
    score_scale = 1.0 / math.sqrt(dim)
    tile_total = lax.axis_size("dp")
    here = lax.axis_index("dp")
    slab, t, h = here // 4, here // 2 % 2, here % 2
    far = jnp.where(slab % 2 == 0, slab - 1, slab + 1)
    listed = partners[0]

    def flags_of(*spots):
        ids = jnp.stack([4 * s + 2 * (t ^ dt) + (h ^ dc) for s, dt, dc in spots])
        inside = jnp.logical_and(ids >= 0, ids < tile_total)
        return jnp.logical_and(
            inside, jnp.any(listed[None, :] == ids[:, None], axis=1)
        ).astype(jnp.int32)

    (w_local,) = call(
        pack_kernel, "pack", [weight.transpose(1, 2, 0, 3)], [((weight.shape[0], columns), BF16)]
    )
    share_height = weight.shape[0]
    half = share_height // 2
    near_pieces, far_pieces = [], []
    for stream in range(2):
        piece = w_local[stream * half : (stream + 1) * half][None]
        for step in (3, 2, 1):
            piece = jnp.concatenate([piece, exchange(piece, stream, step)], axis=0)
        near_pieces.append(piece)
    far_pieces = [exchange(piece, stream, 0) for stream, piece in enumerate(near_pieces)]
    pieces = []
    for stream in range(2):
        pieces += [near_pieces[stream], far_pieces[stream]]
    pieces += [move(piece, CORE) for piece in pieces]
    place_of = jnp.concatenate(
        [
            (reach(here // 2, ORDERS[stream], core) * 2 + core) * share_height + stream * half
            for core in (h, 1 - h)
            for stream in range(2)
        ]
    ).astype(jnp.int32)

    tokens, tile_anchor, *near_pieces = after(tokens, tile_anchor, *near_pieces)
    unit_rows = normalize(tokens)
    normed = (unit_rows * (1.0 + mod_scale) + mod_shift).astype(BF16)
    tables = rope_tables(tile_anchor[0], dim)
    head_at = lax.axis_index("head")
    chip_order = jnp.concatenate([reach(here // 2, ORDERS[n], h) for n in range(2)])
    head_order = reach(head_at, HEAD_ORDERS, h)
    tokens_share = lax.dynamic_slice_in_dim(tokens, head_at * (rows // 4), rows // 4, 0)
    by_owner = normed.T.reshape(16, 2, weight.shape[0], rows)
    mine = lax.dynamic_index_in_dim(by_owner, h, 1, keepdims=False)
    other = move(lax.dynamic_index_in_dim(by_owner, 1 - h, 1, keepdims=False), CORE)
    grad = grad_out.transpose(1, 0, 2)
    normed, mine, other, grad, tokens_share, *tables = after(
        normed, mine, other, grad, tokens_share, *tables
    )

    q, own, raw, w_whole = project(
        place_of, normed, pieces, tables, q_gain, k_gain, heads, dim, score_scale * LOG2E
    )

    pal = slab ^ 1
    f_own = flags_of((slab, 0, 0), (slab, 0, 1))
    f_side = flags_of((slab, 1, 0), (slab, 1, 1))
    f_near = flags_of((pal, 1, 0), (pal, 1, 1))
    f_near1 = flags_of((pal, 0, 0), (pal, 0, 1))
    f_edge = flags_of((far, 1, 0), (far, 1, 1))
    f_edge1 = flags_of((far, 0, 0), (far, 0, 1))
    join = lambda *f: jnp.concatenate(f)

    edge = move(own, HALO)
    side = move(own, Z1)
    own_c = move(own, CORE)
    (acc,) = attend(f_own, q, [own, own_c])
    edge, acc, own_then = after(edge, acc, own)
    near = move(own_then, Z3)
    edge1 = move(edge, Z1)
    edge_c = move(edge, CORE)
    side_c = move(side, CORE)
    (acc,) = attend(join(f_edge, f_side), q, [edge, edge_c, side, side_c], acc)
    near, acc = after(near, acc)
    near1 = move(jnp.where(h == 0, near, side), ACROSS)
    near_c = move(near, CORE)
    edge1_c = move(edge1, CORE)
    (acc,) = attend(join(f_near, f_edge1), q, [near, near_c, edge1, edge1_c], acc)
    near1, acc = after(near1, acc)
    near1_c = move(near1, CORE)
    (acc,) = attend(f_near1[:1], q, [near1], acc)
    attn_out, grad_ext = attend(f_near1[1:], q, [near1_c], acc, grad)

    dq, (d_near1_c,) = differentiate(f_near1[1:], q, grad_ext, [near1_c])
    near1_swap = move(d_near1_c, CORE)
    dq, (d_near1,) = differentiate(f_near1[:1], q, grad_ext, [near1], dq)
    near1_sum = added(d_near1, near1_swap)
    near1_back = move(near1_sum, ACROSS)
    near1_sum, dq = after(near1_sum, dq)
    dq, (d_near, d_near_c) = differentiate(f_near, q, grad_ext, [near, near_c], dq)
    near_swap = move(d_near_c, CORE)
    dq, (d_edge1, d_edge1_c) = differentiate(f_edge1, q, grad_ext, [edge1, edge1_c], dq)
    edge1_swap = move(d_edge1_c, CORE)
    near1_back, dq = after(near1_back, dq)
    dq, (d_edge, d_edge_c, d_side, d_side_c) = differentiate(
        join(f_edge, f_side), q, grad_ext, [edge, edge_c, side, side_c], dq, LONG
    )
    edge_swap = move(d_edge_c, CORE)
    side_swap = move(d_side_c, CORE)
    near_swap, edge1_swap, dq = after(near_swap, edge1_swap, dq)
    none = jnp.zeros((), BF16)
    near_sum = added(d_near, near_swap, jnp.where(h == 0, near1_back, none))
    near_back = move(near_sum, Z3)
    edge1_sum = added(d_edge1, edge1_swap)
    edge1_back = move(edge1_sum, Z1)
    near_sum, edge1_sum, dq = after(near_sum, edge1_sum, dq)
    dq, (d_own, d_own_c) = differentiate(f_own, q, grad_ext, [own, own_c], dq)
    near_back, edge1_back, edge_swap, side_swap, dq, d_own_c = after(
        near_back, edge1_back, edge_swap, side_swap, dq, d_own_c
    )
    edge_sum = added(d_edge, edge_swap, edge1_back)
    edge_back = move(edge_sum, HALO)
    side_sum = added(d_side, side_swap, jnp.where(h == 0, none, near1_back))
    side_back = move(side_sum, Z1)
    own_back = move(d_own_c, CORE)

    grad_proj = pullback(
        raw,
        dq,
        tables,
        q_gain,
        k_gain,
        [d_own, own_back, side_back, near_back, edge_back],
        score_scale,
    )
    grad_proj_other = move(grad_proj, CORE)
    width = weight.shape[0]
    rows_sent, rows_held = input_grad(head_order, grad_proj, w_whole)
    rows_first = head_exchange(rows_sent, 0)
    grad_proj_other, rows_held = after(grad_proj_other, rows_held)

    lhs = [chip_order, mine, other, grad_proj, grad_proj_other]
    shapes = lambda chips, kind: [((chips * width // 2, columns), kind)] * 2
    sent = call(functools.partial(weigh_kernel, 8), "weigh_far", lhs, shapes(8, BF16), smem=1)
    came = [exchange(sent[stream], stream, 0) for stream in range(2)]
    held = call(functools.partial(weigh_kernel, 0), "weigh_near", lhs, shapes(8, F32), smem=1)
    for step in (1, 2, 3):
        *sent, held_a, held_b = call(
            halve_kernel,
            "halve",
            [*held, *came],
            shapes(8 >> step, BF16) + shapes(8 >> step, F32),
        )
        held = [held_a, held_b]
        came = [exchange(sent[stream], stream, step) for stream in range(2)]
        if step == 1:
            rows_first, *held = after(rows_first, *held)
            (rows_next,) = call(
                merge_kernel, "merge_rows", [rows_held, rows_first], [((rows // 4, tokens.shape[1]), BF16)]
            )
            rows_second = head_exchange(rows_next, 1)
            rows_next, *held = after(rows_next, *held)
    (grad_tokens,) = call(
        finish_kernel,
        "finish",
        [rows_held, rows_first, rows_second, tokens_share, mod_scale[None, :]],
        [(tokens_share.shape, BF16)],
    )
    grad_tokens, *held = after(grad_tokens, *held)
    (grad_weight,) = call(
        settle_kernel, "settle", [*held, *came], [((heads, 3, width, dim), F32)]
    )
    return (
        attn_out.transpose(1, 0, 2),
        grad_tokens,
        grad_weight.transpose(2, 0, 1, 3),
    )


def solution(mesh):
    return jax.shard_map(
        local,
        mesh=mesh,
        in_specs=(
            P("dp", None),
            P("dp", None),
            P("dp", None),
            P("dp", "head", None, None),
            P(),
            P(),
            P(),
            P(),
            P("dp", "head", None),
        ),
        out_specs=(P("dp", "head", None), P(("dp", "head"), None), P("dp", "head", None, None)),
        check_vma=False,
    )
```
